512 devices in a mesh: seq: 128 (over y, z, x_lo), head: 4 (over x_hi, core).
Axes of the slice: x: 4 (x_hi: 2, x_lo: 2; x = x_hi * 2 + x_lo), y: 4, z: 16, core: 2. Of those that a mesh axis runs over, the one named last changes fastest.
Arguments:
- self_query: bfloat16 [32768, 1536], P('seq', 'head'), may hold values from -12 to 12
- self_key: bfloat16 [32768, 1536], P('seq', 'head'), may hold values from -12 to 12
- self_value: bfloat16 [32768, 1536], P('seq', 'head'), may hold values from -6 to 6
- cross_query: bfloat16 [32768, 1536], P('seq', 'head'), may hold values from -12 to 12
- cross_key: bfloat16 [32768, 1536], P('seq', 'head'), may hold values from -12 to 12
- cross_value: bfloat16 [32768, 1536], P('seq', 'head'), may hold values from -6 to 6
- cotangent: bfloat16 [32768, 1536], P('seq', 'head'), may hold values from -6 to 6
- norm_gains: float32 [2, 4, 1536], P(None, None, 'head'), may hold values from 0.65 to 1.9
- cross_span: int32 [384, 2], replicated, may hold values from 0 to 4, as said below
Outputs:
- attention_out: bfloat16 [32768, 1536], P('seq', 'head')
- self_query_grad: bfloat16 [32768, 1536], P('seq', 'head')
- self_key_grad: bfloat16 [32768, 1536], P('seq', 'head')
- self_value_grad: bfloat16 [32768, 1536], P('seq', 'head')
- cross_query_grad: bfloat16 [32768, 1536], P('seq', 'head')
- cross_key_grad: bfloat16 [32768, 1536], P('seq', 'head')
- cross_value_grad: bfloat16 [32768, 1536], P('seq', 'head')
The draws below stay inside these ranges and needn't reach their ends.
Inputs may be any that keep to these rules, and one draw needn't show every extreme that they name: `cross_span`: row b gives a range lo to hi of 64-token blocks inside the audio block aligned in time with video block b // 4; always lo <= b % 4 < hi.
All inputs are finite; a program needn't handle non-finite values.
Results may differ from the reference program's by a relative error of at most 0.013.
The reference program's roundings to bfloat16 on the way count: a program that leaves them out, or rounds other values in their place, can miss the bound.
Values may be sent and summed in bfloat16 or wider, within the bound.
No kernel may reach another device: no remote copies, remote signals or barrier semaphores. Data moves between devices by JAX's collectives and lax.ppermute only.
A program may use at most 64 MiB of HBM per device.

```python
import math
import jax
import jax.numpy as jnp
from jax import lax

TOKENS_PER_SHARD = 256
DH = 128
BLK = 64
REACH = 1
WIDTH = 1536
NSUB = 4
TOKENS = 32768
VIDEO = 24576
VBLOCKS = 384
N_SEQ = 128


def scaled_field(key, entries, lowest, highest):
    key_rows, key_cols = jax.random.split(key)
    row_scale = jnp.exp(jax.random.uniform(key_rows, (TOKENS, 1), minval=math.log(lowest), maxval=math.log(highest)))
    col_scale = jnp.exp(jax.random.uniform(key_cols, (1, WIDTH), minval=math.log(lowest), maxval=math.log(highest)))
    return entries * row_scale * col_scale


def drawn_pair(key, stream):
    key = jax.random.fold_in(key, stream)
    key_qa, key_ka, key_qs, key_ks = jax.random.split(key, 4)
    queries = scaled_field(key_qs, jax.random.normal(key_qa, (TOKENS, WIDTH)), 0.5, 2.0)
    keys = scaled_field(key_ks, jax.random.normal(key_ka, (TOKENS, WIDTH)), 0.5, 2.0)
    return (jnp.clip(queries, -12.0, 12.0), jnp.clip(keys, -12.0, 12.0))


def draw_self_query(key, part):
    return drawn_pair(key, 11)[0].astype(jnp.bfloat16)


def draw_self_key(key, part):
    return drawn_pair(key, 11)[1].astype(jnp.bfloat16)


def draw_cross_query(key, part):
    return drawn_pair(key, 12)[0].astype(jnp.bfloat16)


def draw_cross_key(key, part):
    return drawn_pair(key, 12)[1].astype(jnp.bfloat16)


def draw_norm_gains(key, part):
    key = jax.random.fold_in(key, 31)
    gains = 1.0 + 0.35 * jax.random.uniform(key, (2, 4, WIDTH), minval=-1.0, maxval=1.0)
    return gains.astype(jnp.float32)


def draw_cross_span(key, part):
    key = jax.random.fold_in(key, 41)
    key_lower, key_upper = jax.random.split(key)
    within = jnp.arange(VBLOCKS, dtype=jnp.int32) % NSUB
    lower_end = jax.random.randint(key_lower, (VBLOCKS,), 0, within + 1)
    upper_end = jax.random.randint(key_upper, (VBLOCKS,), within + 1, NSUB + 1)
    return jnp.stack([lower_end, upper_end], axis=1).astype(jnp.int32)


def level_of(own_key, extent, cuts, smallest, largest):
    def one(dim, parts):
        heights = jax.random.uniform(jax.random.fold_in(jax.random.fold_in(own_key, 6), dim), (parts,), jnp.float32, smallest / len(cuts), largest / len(cuts))
        return jnp.repeat(jnp.exp(heights), extent[dim] // parts).reshape((-1,) + (1,) * (len(extent) - dim - 1))

    gain = one(*cuts[0])
    for cut in cuts[1:]:
        gain = gain * one(*cut)
    return gain


def normal_values(own_key, dims, width, most, shards=(), held_as=jnp.bfloat16):
    values = jax.random.normal(own_key, dims, jnp.float32) * width
    if len(shards) > 0:
        values = level_of(own_key, dims, shards, -0.22, 0.18) * values
    return jnp.clip(values, min=-most, max=most).astype(held_as)


def setup_inputs(seed: int = 0) -> dict:
    splits = jax.random.split(jax.random.key(seed), 10)
    return {
        "self_query": draw_self_query(jax.random.fold_in(splits[9], 71), 0),
        "self_key": draw_self_key(jax.random.fold_in(splits[9], 71), 0),
        "self_value": normal_values(splits[2], (TOKENS, WIDTH), 1.0, 6.0, ((0, 128), (1, 4))),
        "cross_query": draw_cross_query(jax.random.fold_in(splits[9], 71), 0),
        "cross_key": draw_cross_key(jax.random.fold_in(splits[9], 71), 0),
        "cross_value": normal_values(splits[5], (TOKENS, WIDTH), 1.0, 6.0, ((0, 128), (1, 4))),
        "cotangent": normal_values(splits[6], (TOKENS, WIDTH), 1.0, 6.0, ((0, 128), (1, 4))),
        "norm_gains": draw_norm_gains(jax.random.fold_in(splits[9], 71), 0),
        "cross_span": draw_cross_span(jax.random.fold_in(splits[9], 71), 0),
    }


EPSILON = 1e-06

def split_heads(tensor):
    return tensor.reshape(tensor.shape[0], tensor.shape[1] // DH, DH).astype(jnp.float32)

def query_side(queries, keys, values, upstream, allowed):
    tok_rows = queries.shape[0]
    scores = jnp.einsum('qhd,khd->hqk', split_heads(queries), split_heads(keys)) * DH ** (-0.5)
    scores = jnp.where(allowed[None], scores, -jnp.inf)
    row_max = lax.optimization_barrier(jnp.max(scores, axis=2))
    shifted = jnp.exp(scores - row_max[:, :, None])
    row_total = lax.optimization_barrier(jnp.sum(shifted, axis=2))
    soft_probs = shifted / row_total[:, :, None]
    weights = lax.optimization_barrier(soft_probs.astype(jnp.bfloat16)).astype(jnp.float32)
    value_heads = split_heads(values)
    grad_heads = split_heads(upstream)
    result = jnp.einsum('hqk,khd->qhd', weights, value_heads).reshape(tok_rows, -1)
    prob_grad = jnp.einsum('qhd,khd->hqk', grad_heads, value_heads)
    row_delta = lax.optimization_barrier(jnp.sum(soft_probs * prob_grad, axis=2))
    score_grad = (soft_probs * (prob_grad - row_delta[:, :, None]) * DH ** (-0.5)).astype(jnp.bfloat16)
    score_grad = lax.optimization_barrier(score_grad).astype(jnp.float32)
    query_grad = jnp.einsum('hqk,khd->qhd', score_grad, split_heads(keys)).reshape(tok_rows, -1)
    key_grad = jnp.einsum('hqk,qhd->khd', score_grad, split_heads(queries)).reshape(keys.shape[0], -1)
    value_grad = jnp.einsum('hqk,qhd->khd', weights, grad_heads).reshape(keys.shape[0], -1)
    return (result, query_grad, key_grad, value_grad)

def cross_mask(my_index, receipt, cross_span, quarter):
    my_group = my_index // quarter
    sender_device = (my_index - receipt * quarter) % (4 * quarter)
    own_span = lax.dynamic_slice_in_dim(cross_span, (jnp.minimum(my_index, 3 * quarter - 1) * NSUB).astype(jnp.int32), NSUB, 0)
    their_span = lax.dynamic_slice_in_dim(cross_span, (jnp.minimum(sender_device, 3 * quarter - 1) * NSUB).astype(jnp.int32), NSUB, 0)
    sub_index = jnp.arange(NSUB * BLK, dtype=jnp.int32) // BLK
    own_lower = jnp.repeat(own_span[:, 0], BLK)[:, None]
    own_upper = jnp.repeat(own_span[:, 1], BLK)[:, None]
    their_lower = jnp.repeat(their_span[:, 0], BLK)[None, :]
    their_upper = jnp.repeat(their_span[:, 1], BLK)[None, :]
    video_side = (my_group < 3) & (sender_device // quarter == 3) & (own_lower <= sub_index[None, :]) & (sub_index[None, :] < own_upper)
    audio_side = (my_group == 3) & (sender_device // quarter < 3) & (their_lower <= sub_index[:, None]) & (sub_index[:, None] < their_upper)
    return video_side | audio_side

def reference(self_query, self_key, self_value, cross_query, cross_key, cross_value, cotangent, norm_gains, cross_span):
    quarter = N_SEQ // 4
    is_audio = (jnp.arange(TOKENS, dtype=jnp.int32) >= VIDEO)[:, None]
    inputs = (self_query, self_key, cross_query, cross_key)
    normed = []
    scales = []
    gain_list = []
    for which in range(4):
        gain_rows = jnp.where(is_audio, norm_gains[1, which][None, :], norm_gains[0, which][None, :])
        wide = inputs[which].astype(jnp.float32)
        inv_rms = lax.rsqrt(lax.optimization_barrier(jnp.mean(wide * wide, axis=1)) + EPSILON)
        normed.append((wide * inv_rms[:, None] * gain_rows).astype(jnp.bfloat16).reshape(N_SEQ, TOKENS_PER_SHARD, WIDTH))
        scales.append(inv_rms)
        gain_list.append(gain_rows)
    value_self = self_value.reshape(N_SEQ, TOKENS_PER_SHARD, WIDTH)
    value_cross = cross_value.reshape(N_SEQ, TOKENS_PER_SHARD, WIDTH)
    grad_blocks = cotangent.reshape(N_SEQ, TOKENS_PER_SHARD, WIDTH)
    offsets = list(range(-REACH, REACH + 1))

    def step(loop_carry_state, my_index):
        self_key_accumulator, self_value_accumulator, cross_key_accumulator, cross_value_accumulator = loop_carry_state
        targets = [jnp.clip(my_index + offset, 0, N_SEQ - 1) for offset in offsets]
        slot_valid = jnp.stack([(my_index + offset >= 0) & (my_index + offset < N_SEQ) & ((my_index + offset) // quarter == my_index // quarter) for offset in offsets])
        keys = jnp.concatenate([normed[1][receiver_device] for receiver_device in targets])
        values = jnp.concatenate([value_self[receiver_device] for receiver_device in targets])
        allowed = jnp.broadcast_to(jnp.repeat(slot_valid, TOKENS_PER_SHARD)[None, :], (TOKENS_PER_SHARD, len(offsets) * TOKENS_PER_SHARD))
        self_out, self_qgrad, self_kparts, self_value_pieces = query_side(normed[0][my_index], keys, values, grad_blocks[my_index], allowed)
        for position_index, receiver_device in enumerate(targets):
            self_key_accumulator = self_key_accumulator.at[receiver_device].add(self_kparts[position_index * TOKENS_PER_SHARD:(position_index + 1) * TOKENS_PER_SHARD])
            self_value_accumulator = self_value_accumulator.at[receiver_device].add(self_value_pieces[position_index * TOKENS_PER_SHARD:(position_index + 1) * TOKENS_PER_SHARD])
        sources = [(my_index - receipt * quarter) % N_SEQ for receipt in range(1, 4)]
        cross_keys = jnp.concatenate([normed[3][sender_device] for sender_device in sources])
        cross_values = jnp.concatenate([value_cross[sender_device] for sender_device in sources])
        cross_allowed = jnp.concatenate([cross_mask(my_index, receipt, cross_span, quarter) for receipt in range(1, 4)], axis=1)
        cross_out, cross_qgrad, cross_kparts, cross_value_pieces = query_side(normed[2][my_index], cross_keys, cross_values, grad_blocks[my_index], cross_allowed)
        for position_index, sender_device in enumerate(sources):
            cross_key_accumulator = cross_key_accumulator.at[sender_device].add(cross_kparts[position_index * TOKENS_PER_SHARD:(position_index + 1) * TOKENS_PER_SHARD])
            cross_value_accumulator = cross_value_accumulator.at[sender_device].add(cross_value_pieces[position_index * TOKENS_PER_SHARD:(position_index + 1) * TOKENS_PER_SHARD])
        output_list = ((self_out + cross_out).astype(jnp.bfloat16), self_qgrad, cross_qgrad)
        return ((self_key_accumulator, self_value_accumulator, cross_key_accumulator, cross_value_accumulator), output_list)
    start = tuple((jnp.zeros((N_SEQ, TOKENS_PER_SHARD, WIDTH), jnp.float32) for which in range(4)))
    final, stacked = lax.scan(step, start, jnp.arange(N_SEQ, dtype=jnp.int32))
    attention_out = stacked[0].reshape(TOKENS, WIDTH)
    upstream = (stacked[1].reshape(TOKENS, WIDTH), final[0].reshape(TOKENS, WIDTH), stacked[2].reshape(TOKENS, WIDTH), final[2].reshape(TOKENS, WIDTH))
    results = []
    for which in range(4):
        wide = inputs[which].astype(jnp.float32)
        inner = lax.optimization_barrier(jnp.mean(gain_list[which] * upstream[which] * wide, axis=1))
        inv_rms = scales[which]
        results.append((inv_rms[:, None] * gain_list[which] * upstream[which] - wide * (inv_rms ** 3 * inner)[:, None]).astype(jnp.bfloat16))
    self_value_grad = final[1].reshape(TOKENS, WIDTH).astype(jnp.bfloat16)
    cross_value_grad = final[3].reshape(TOKENS, WIDTH).astype(jnp.bfloat16)
    return (attention_out, results[0], results[1], self_value_grad, results[2], results[3], cross_value_grad)
```

```python
import functools

import jax
import jax.numpy as jnp
from jax import lax
from jax.experimental import pallas as pl
from jax.experimental.pallas import tpu as pltpu
from jax.sharding import Mesh, PartitionSpec as P

DH = 128
BLK = 64
WIDTH = 1536
NSUB = 4
HEADS = 3
TOK = 256
COLS = 384
EPSILON = 1e-06
SCALE = DH ** (-0.5)
MASKED = -1e30
F32 = jnp.float32
BF16 = jnp.bfloat16
VMEM = pltpu.VMEM
VSPEC = pl.BlockSpec(memory_space=pltpu.VMEM)
SSPEC = pl.BlockSpec(memory_space=pltpu.SMEM)


def dot(a, b, ca, cb):
    return lax.dot_general(a, b, (((ca,), (cb,)), ((), ())), preferred_element_type=F32)


def row_sums(product):
    folded = product[:, 0:128] + product[:, 128:256] + product[:, 256:384]
    return jnp.sum(jnp.transpose(folded), axis=0, keepdims=True)


def squares_kernel(*refs):
    ins, out = refs[:-1], refs[-1]
    out[...] = jnp.zeros(out.shape, F32)
    for i, ref in enumerate(ins):
        wide = ref[...].astype(F32)
        out[i : i + 1, :] = row_sums(wide * wide)


def attend(heads_q, heads_k, heads_v, heads_do, biases, masks):
    scores = []
    for kn, bias, mask in zip(heads_k, biases, masks):
        s = dot(kn, heads_q, 1, 1)
        if bias is not None:
            s = s + bias
        if mask is not None:
            s = jnp.where(mask, s, MASKED)
        scores.append(s)
    top = functools.reduce(jnp.maximum, [jnp.max(s, axis=0, keepdims=True) for s in scores])
    shifted = [jnp.exp((s - top) * SCALE) for s in scores]
    total = sum(jnp.sum(e, axis=0, keepdims=True) for e in shifted)
    inverse = 1.0 / total
    probs = [e * inverse for e in shifted]
    dprobs = [dot(v, heads_do, 1, 1) for v in heads_v]
    delta = sum(jnp.sum(p * d, axis=0, keepdims=True) for p, d in zip(probs, dprobs))
    out = dq = None
    dks, dvs = [], []
    for p, d, kn, v in zip(probs, dprobs, heads_k, heads_v):
        w = p.astype(BF16)
        ds = (p * (d - delta) * SCALE).astype(BF16)
        o_part = dot(w, v, 0, 0)
        q_part = dot(ds, kn, 0, 0)
        out = o_part if out is None else out + o_part
        dq = q_part if dq is None else dq + q_part
        dks.append(dot(ds, heads_q, 1, 0))
        dvs.append(dot(w, heads_do, 1, 0))
    return out, dq, dks, dvs


def inverse_rms(sums_ref):
    return jnp.transpose(lax.rsqrt(sums_ref[...] * (1.0 / WIDTH) + EPSILON))


def normed(raw, inv, gain):
    return (raw.astype(F32) * inv * gain).astype(BF16)


def self_kernel(
    scal, sums, gains, q_ref, k_ref, v_ref, do_ref, kb_ref, vb_ref, ka_ref, va_ref,
    out_ref, dq_ref, dk_ref, dv_ref, pb_ref, pa_ref,
):
    group, slot = scal[0], scal[1]
    tower = (group == 3).astype(jnp.int32)
    inv = inverse_rms(sums)
    bias_b = jnp.where(slot > 0, 0.0, MASKED).astype(F32)
    bias_a = jnp.where(slot < 31, 0.0, MASKED).astype(F32)
    for h in range(HEADS):
        c = slice(h * DH, (h + 1) * DH)
        gq = gains[tower, 0:1, c]
        gk = gains[tower, 1:2, c]
        qn = normed(q_ref[:, c], inv[:, 0:1], gq)
        do = do_ref[:, c]
        kn = [
            normed(k_ref[:, c], inv[:, 1:2], gk),
            normed(kb_ref[:, c], inv[:, 4:5], gk),
            normed(ka_ref[:, c], inv[:, 5:6], gk),
        ]
        vs = [v_ref[:, c], vb_ref[:, c], va_ref[:, c]]
        out, dq, dks, dvs = attend(qn, kn, vs, do, [None, bias_b, bias_a], [None] * 3)
        out_ref[:, c] = out
        dq_ref[:, c] = dq
        dk_ref[:, c] = dks[0]
        dv_ref[:, c] = dvs[0]
        for ref, i in ((pb_ref, 1), (pa_ref, 2)):
            ref[0:TOK, c] = dks[i].astype(BF16)
            ref[TOK:, c] = dvs[i].astype(BF16)


def cross_kernel(
    scal, sums, gains, q_ref, do_ref, k0, v0, k1, v1, k2, v2,
    out_ref, dq_ref, p0, p1, p2,
):
    group = scal[0]
    audio = group == 3
    inv = inverse_rms(sums)
    sub_row = lax.broadcasted_iota(jnp.int32, (1, TOK), 1) // BLK
    sub_col = lax.broadcasted_iota(jnp.int32, (TOK, 1), 0) // BLK

    def spread(base, offset, sub):
        value = jnp.zeros(sub.shape, jnp.int32)
        for b in range(NSUB):
            value = jnp.where(sub == b, scal[base + 2 * b + offset], value)
        return value

    @pl.when(audio)
    def _():
        masks = []
        for j in range(3):
            lower = spread(2 + 8 * j, 0, sub_col)
            upper = spread(2 + 8 * j, 1, sub_col)
            masks.append((sub_row >= lower) & (sub_row < upper))
        for h in range(HEADS):
            c = slice(h * DH, (h + 1) * DH)
            qn = normed(q_ref[:, c], inv[:, 2:3], gains[1, 2:3, c])
            do = do_ref[:, c]
            kn = [normed(k[:, c], inv[:, 6 + j : 7 + j], gains[0, 3:4, c]) for j, k in enumerate((k0, k1, k2))]
            vs = [v[:, c] for v in (v0, v1, v2)]
            out, dq, dks, dvs = attend(qn, kn, vs, do, [None] * 3, masks)
            out_ref[:, c] = out
            dq_ref[:, c] = dq
            for ref, dk, dv in zip((p0, p1, p2), dks, dvs):
                ref[0:TOK, c] = dk.astype(BF16)
                ref[TOK:, c] = dv.astype(BF16)

    @pl.when(jnp.logical_not(audio))
    def _():
        base = 2 + 8 * group
        lower = spread(base, 0, sub_row)
        upper = spread(base, 1, sub_row)
        mask = (sub_col >= lower) & (sub_col < upper)
        first, second = group == 0, group == 1

        def pick(a, b, c):
            return jnp.where(first, a, jnp.where(second, b, c))

        inv_k = pick(inv[:, 6:7], inv[:, 7:8], inv[:, 8:9])
        for h in range(HEADS):
            c = slice(h * DH, (h + 1) * DH)
            qn = normed(q_ref[:, c], inv[:, 2:3], gains[0, 2:3, c])
            do = do_ref[:, c]
            kn = normed(pick(k0[:, c], k1[:, c], k2[:, c]), inv_k, gains[1, 3:4, c])
            v = pick(v0[:, c], v1[:, c], v2[:, c])
            out, dq, dks, dvs = attend(qn, [kn], [v], do, [None], [mask])
            out_ref[:, c] = out
            dq_ref[:, c] = dq
            dk = dks[0].astype(BF16)
            dv = dvs[0].astype(BF16)
            for j, ref in enumerate((p0, p1, p2)):

                @pl.when(group == j)
                def _():
                    ref[0:TOK, c] = dk
                    ref[TOK:, c] = dv


def gather_kernel(
    scal, gains, sq, sk, cq, ck, so, co, sdq, cdq, sdk, sdv, rb, ra, r0, r1, r2,
    att, svg, cvg, dks_ref, dkc_ref, inner,
):
    tower = (scal[0] == 3).astype(jnp.int32)
    att[...] = (so[...] + co[...]).astype(BF16)
    dks = sdk[...] + rb[0:TOK, :].astype(F32) + ra[0:TOK, :].astype(F32)
    svg[...] = (sdv[...] + rb[TOK:, :].astype(F32) + ra[TOK:, :].astype(F32)).astype(BF16)
    dkc = r0[0:TOK, :].astype(F32) + r1[0:TOK, :].astype(F32) + r2[0:TOK, :].astype(F32)
    cvg[...] = (r0[TOK:, :].astype(F32) + r1[TOK:, :].astype(F32) + r2[TOK:, :].astype(F32)).astype(BF16)
    dks_ref[...] = dks
    dkc_ref[...] = dkc
    inner[...] = jnp.zeros(inner.shape, F32)
    for i, (x, y) in enumerate(((sq, sdq[...]), (sk, dks), (cq, cdq[...]), (ck, dkc))):
        inner[i : i + 1, :] = row_sums(gains[tower, i : i + 1, :] * y * x[...].astype(F32))


def final_kernel(scal, gains, sums, inner, sq, sk, cq, ck, y0, y1, y2, y3, o0, o1, o2, o3):
    tower = (scal[0] == 3).astype(jnp.int32)
    inv = inverse_rms(sums)
    mean = jnp.transpose(inner[...]) * (1.0 / WIDTH)
    for i, (x, y, o) in enumerate(zip((sq, sk, cq, ck), (y0, y1, y2, y3), (o0, o1, o2, o3))):
        r = inv[:, i : i + 1]
        o[...] = (
            r * gains[tower, i : i + 1, :] * y[...] - x[...].astype(F32) * (r * r * r * mean[:, i : i + 1])
        ).astype(BF16)


def shape(rows, dtype, cols=COLS):
    return jax.ShapeDtypeStruct((rows, cols), dtype)


def call(kernel, name, scalars, outs, *args, flops=0):
    nbytes = sum(a.size * a.dtype.itemsize for a in args) + sum(o.size * o.dtype.itemsize for o in outs)
    return pl.pallas_call(
        kernel,
        name=name,
        out_shape=outs,
        in_specs=[SSPEC] * scalars + [VSPEC] * (len(args) - scalars),
        out_specs=[VSPEC] * len(outs),
        compiler_params=pltpu.CompilerParams(vmem_limit_bytes=40 * 1024 * 1024),
        cost_estimate=pl.CostEstimate(flops=flops, bytes_accessed=nbytes, transcendentals=0),
    )(*args)


def on_device(sq, sk, sv, cq, ck, cv, do, gains, span):
    group = lax.axis_index("y")
    slot = lax.axis_index("t")
    slots = lax.axis_size("t")
    up = [(i, i + 1) for i in range(slots - 1)]
    down = [(i + 1, i) for i in range(slots - 1)]
    pairs = [[(3, j), (j, 3)] for j in range(3)]
    spans = lax.dynamic_slice_in_dim(span.reshape(3, NSUB * slots, 2), slot * NSUB, NSUB, 1)
    scal = jnp.concatenate([jnp.stack([group, slot]).astype(jnp.int32), spans.reshape(-1)])

    c_in = [(lax.ppermute(ck, "y", p), lax.ppermute(cv, "y", p)) for p in pairs]
    kb, vb = lax.ppermute(sk, "t", up), lax.ppermute(sv, "t", up)
    ka, va = lax.ppermute(sk, "t", down), lax.ppermute(sv, "t", down)

    sums = call(
        squares_kernel, "squares", 0, [shape(16, F32, TOK)], sq, sk, cq, ck, kb, ka, c_in[0][0], c_in[1][0], c_in[2][0]
    )[0]
    sums = lax.psum(sums, "head")

    flat = [a for pair in c_in for a in pair]
    c_out, c_dq, *c_parts = call(
        cross_kernel, "cross", 1, [shape(TOK, F32)] * 2 + [shape(2 * TOK, BF16)] * 3, scal, sums, gains, cq, do, *flat,
        flops=12 * HEADS * TOK * 3 * TOK * DH,
    )
    c_back = [lax.ppermute(part, "y", p) for part, p in zip(c_parts, pairs)]
    s_out, s_dq, s_dk, s_dv, part_b, part_a = call(
        self_kernel, "selfatt", 1, [shape(TOK, F32)] * 4 + [shape(2 * TOK, BF16)] * 2, scal, sums, gains, sq, sk, sv, do,
        kb, vb, ka, va, flops=12 * HEADS * TOK * 3 * TOK * DH,
    )
    back_a = lax.ppermute(part_b, "t", down)
    back_b = lax.ppermute(part_a, "t", up)

    att, svg, cvg, dks, dkc, inner = call(
        gather_kernel, "gather", 1, [shape(TOK, BF16)] * 3 + [shape(TOK, F32)] * 2 + [shape(8, F32, TOK)],
        scal, gains, sq, sk, cq, ck, s_out, c_out, s_dq, c_dq, s_dk, s_dv, back_b, back_a, *c_back,
    )
    inner = lax.psum(inner, "head")
    g0, g1, g2, g3 = call(
        final_kernel, "final", 1, [shape(TOK, BF16)] * 4, scal, gains, sums, inner, sq, sk, cq, ck, s_dq, dks, c_dq, dkc
    )
    return att, g0, g1, svg, g2, g3, cvg


def solution(mesh):
    seq = mesh.shape["seq"]
    grid = Mesh(mesh.devices.reshape(4, seq // 4, mesh.shape["head"]), ("y", "t", "head"))
    block = P(("y", "t"), "head")
    return jax.shard_map(
        on_device,
        mesh=grid,
        in_specs=(block,) * 7 + (P(None, None, "head"), P()),
        out_specs=(block,) * 7,
        check_vma=False,
    )
```

```python
import functools

import jax
import jax.numpy as jnp
from jax import lax
from jax.experimental import pallas as pl
from jax.experimental.pallas import tpu as pltpu
from jax.sharding import Mesh, PartitionSpec as P

DH = 128
BLK = 64
WIDTH = 1536
NSUB = 4
HEADS = 3
TOK = 256
COLS = 384
EPSILON = 1e-06
SCALE = DH ** (-0.5)
MASKED = -1e30
F32 = jnp.float32
BF16 = jnp.bfloat16
VMEM = pltpu.VMEM
VSPEC = pl.BlockSpec(memory_space=pltpu.VMEM)
SSPEC = pl.BlockSpec(memory_space=pltpu.SMEM)


def dot(a, b, ca, cb):
    return lax.dot_general(a, b, (((ca,), (cb,)), ((), ())), preferred_element_type=F32)


def row_sums(product):
    folded = product[:, 0:128] + product[:, 128:256] + product[:, 256:384]
    return jnp.sum(jnp.transpose(folded), axis=0, keepdims=True)


def squares_kernel(*refs):
    ins, out = refs[:-1], refs[-1]
    out[...] = jnp.zeros(out.shape, F32)
    for i, ref in enumerate(ins):
        wide = ref[0:TOK, :].astype(F32)
        out[i : i + 1, :] = row_sums(wide * wide)


def more_squares_kernel(own, *refs):
    ins, out = refs[:-1], refs[-1]
    out[0:8, :] = own[...]
    out[8:16, :] = jnp.zeros((8, TOK), F32)
    for i, ref in enumerate(ins):
        wide = ref[0:TOK, :].astype(F32)
        row = (8, 4, 6, 7, 5)[i]
        out[row : row + 1, :] = row_sums(wide * wide)


def attend(heads_q, heads_k, heads_v, heads_do, biases, masks):
    scores = []
    for kn, bias, mask in zip(heads_k, biases, masks):
        s = dot(kn, heads_q, 1, 1)
        if bias is not None:
            s = s + bias
        if mask is not None:
            s = jnp.where(mask, s, MASKED)
        scores.append(s)
    top = functools.reduce(jnp.maximum, [jnp.max(s, axis=0, keepdims=True) for s in scores])
    shifted = [jnp.exp((s - top) * SCALE) for s in scores]
    total = sum(jnp.sum(e, axis=0, keepdims=True) for e in shifted)
    inverse = 1.0 / total
    probs = [e * inverse for e in shifted]
    dprobs = [dot(v, heads_do, 1, 1) for v in heads_v]
    delta = sum(jnp.sum(p * d, axis=0, keepdims=True) for p, d in zip(probs, dprobs))
    out = dq = None
    dks, dvs = [], []
    for p, d, kn, v in zip(probs, dprobs, heads_k, heads_v):
        w = p.astype(BF16)
        ds = (p * (d - delta) * SCALE).astype(BF16)
        o_part = dot(w, v, 0, 0)
        q_part = dot(ds, kn, 0, 0)
        out = o_part if out is None else out + o_part
        dq = q_part if dq is None else dq + q_part
        dks.append(dot(ds, heads_q, 1, 0))
        dvs.append(dot(w, heads_do, 1, 0))
    return out, dq, dks, dvs


def over_heads(ref):
    return ref[0] + ref[1] + ref[2] + ref[3]


def inverse_rms(sums_ref):
    return jnp.transpose(lax.rsqrt(over_heads(sums_ref) * (1.0 / WIDTH) + EPSILON))


def normed(raw, inv, gain):
    return (raw.astype(F32) * inv * gain).astype(BF16)


def self_kernel(
    scal, sums, gains, q_ref, k_ref, v_ref, do_ref, b_ref, a_ref,
    out_ref, dq_ref, dk_ref, dv_ref, pb_ref, pa_ref,
):
    group, slot = scal[0], scal[1]
    tower = (group == 3).astype(jnp.int32)
    inv = inverse_rms(sums)
    bias_b = jnp.where(slot > 0, 0.0, MASKED).astype(F32)
    bias_a = jnp.where(slot < 31, 0.0, MASKED).astype(F32)
    for h in range(HEADS):
        c = slice(h * DH, (h + 1) * DH)
        gq = gains[tower, 0:1, c]
        gk = gains[tower, 1:2, c]
        qn = normed(q_ref[:, c], inv[:, 0:1], gq)
        do = do_ref[:, c]
        kn = [
            normed(k_ref[:, c], inv[:, 1:2], gk),
            normed(b_ref[0:TOK, c], inv[:, 4:5], gk),
            normed(a_ref[0:TOK, c], inv[:, 5:6], gk),
        ]
        vs = [v_ref[:, c], b_ref[TOK:, c], a_ref[TOK:, c]]
        out, dq, dks, dvs = attend(qn, kn, vs, do, [None, bias_b, bias_a], [None] * 3)
        out_ref[:, c] = out
        dq_ref[:, c] = dq
        dk_ref[:, c] = dks[0]
        dv_ref[:, c] = dvs[0]
        for ref, i in ((pb_ref, 1), (pa_ref, 2)):
            ref[0:TOK, c] = dks[i].astype(BF16)
            ref[TOK:, c] = dvs[i].astype(BF16)


def cross_kernel(
    scal, sums, gains, q_ref, do_ref, i0, i1, i2, s_ref,
    out_ref, dq_ref, p0, p1, p2,
):
    group = scal[0]
    audio = group == 3
    inv = inverse_rms(sums)
    sub_row = lax.broadcasted_iota(jnp.int32, (1, TOK), 1) // BLK
    sub_col = lax.broadcasted_iota(jnp.int32, (TOK, 1), 0) // BLK

    def spread(base, offset, sub):
        value = jnp.zeros(sub.shape, jnp.int32)
        for b in range(NSUB):
            value = jnp.where(sub == b, scal[base + 2 * b + offset], value)
        return value

    @pl.when(audio)
    def _():
        masks = []
        for j in range(3):
            lower = spread(2 + 8 * j, 0, sub_col)
            upper = spread(2 + 8 * j, 1, sub_col)
            masks.append((sub_row >= lower) & (sub_row < upper))
        for h in range(HEADS):
            c = slice(h * DH, (h + 1) * DH)
            qn = normed(q_ref[:, c], inv[:, 2:3], gains[1, 2:3, c])
            do = do_ref[:, c]
            kn = [normed(r[0:TOK, c], inv[:, 6 + j : 7 + j], gains[0, 3:4, c]) for j, r in enumerate((i0, i1, i2))]
            vs = [r[TOK:, c] for r in (i0, i1, i2)]
            out, dq, dks, dvs = attend(qn, kn, vs, do, [None] * 3, masks)
            out_ref[:, c] = (out + s_ref[:, c]).astype(BF16)
            dq_ref[:, c] = dq
            for ref, dk, dv in zip((p0, p1, p2), dks, dvs):
                ref[0:TOK, c] = dk.astype(BF16)
                ref[TOK:, c] = dv.astype(BF16)

    @pl.when(jnp.logical_not(audio))
    def _():
        base = 2 + 8 * group
        lower = spread(base, 0, sub_row)
        upper = spread(base, 1, sub_row)
        mask = (sub_col >= lower) & (sub_col < upper)
        first, second = group == 0, group == 1

        def pick(a, b, c):
            return jnp.where(first, a, jnp.where(second, b, c))

        inv_k = pick(inv[:, 6:7], inv[:, 7:8], inv[:, 8:9])
        for h in range(HEADS):
            c = slice(h * DH, (h + 1) * DH)
            qn = normed(q_ref[:, c], inv[:, 2:3], gains[0, 2:3, c])
            do = do_ref[:, c]
            kn = normed(pick(i0[0:TOK, c], i1[0:TOK, c], i2[0:TOK, c]), inv_k, gains[1, 3:4, c])
            v = pick(i0[TOK:, c], i1[TOK:, c], i2[TOK:, c])
            out, dq, dks, dvs = attend(qn, [kn], [v], do, [None], [mask])
            out_ref[:, c] = (out + s_ref[:, c]).astype(BF16)
            dq_ref[:, c] = dq
            dk = dks[0].astype(BF16)
            dv = dvs[0].astype(BF16)
            for j, ref in enumerate((p0, p1, p2)):

                @pl.when(group == j)
                def _():
                    ref[0:TOK, c] = dk
                    ref[TOK:, c] = dv


def gather_kernel(
    scal, gains, sq, sk, cq, ck, sdq, cdq, sdk, sdv, rb, r1, r0, r2, ra,
    svg, cvg, dks_ref, dkc_ref, inner,
):
    tower = (scal[0] == 3).astype(jnp.int32)
    dks = sdk[...] + rb[0:TOK, :].astype(F32) + ra[0:TOK, :].astype(F32)
    svg[...] = (sdv[...] + rb[TOK:, :].astype(F32) + ra[TOK:, :].astype(F32)).astype(BF16)
    dkc = r0[0:TOK, :].astype(F32) + r1[0:TOK, :].astype(F32) + r2[0:TOK, :].astype(F32)
    cvg[...] = (r0[TOK:, :].astype(F32) + r1[TOK:, :].astype(F32) + r2[TOK:, :].astype(F32)).astype(BF16)
    dks_ref[...] = dks
    dkc_ref[...] = dkc
    inner[...] = jnp.zeros(inner.shape, F32)
    for i, (x, y) in enumerate(((sq, sdq[...]), (sk, dks), (cq, cdq[...]), (ck, dkc))):
        inner[i : i + 1, :] = row_sums(gains[tower, i : i + 1, :] * y * x[...].astype(F32))


def final_kernel(scal, gains, sums, inner, sq, sk, cq, ck, y0, y1, y2, y3, o0, o1, o2, o3):
    tower = (scal[0] == 3).astype(jnp.int32)
    inv = inverse_rms(sums)
    mean = jnp.transpose(over_heads(inner)) * (1.0 / WIDTH)
    for i, (x, y, o) in enumerate(zip((sq, sk, cq, ck), (y0, y1, y2, y3), (o0, o1, o2, o3))):
        r = inv[:, i : i + 1]
        o[...] = (
            r * gains[tower, i : i + 1, :] * y[...] - x[...].astype(F32) * (r * r * r * mean[:, i : i + 1])
        ).astype(BF16)


def shape(rows, dtype, cols=COLS):
    return jax.ShapeDtypeStruct((rows, cols), dtype)


def call(kernel, name, scalars, outs, *args, flops=0):
    nbytes = sum(a.size * a.dtype.itemsize for a in args) + sum(o.size * o.dtype.itemsize for o in outs)
    return pl.pallas_call(
        kernel,
        name=name,
        out_shape=outs,
        in_specs=[SSPEC] * scalars + [VSPEC] * (len(args) - scalars),
        out_specs=[VSPEC] * len(outs),
        compiler_params=pltpu.CompilerParams(vmem_limit_bytes=40 * 1024 * 1024),
        cost_estimate=pl.CostEstimate(flops=flops, bytes_accessed=nbytes, transcendentals=0),
    )(*args)


def on_device(sq, sk, sv, cq, ck, cv, do, gains, span):
    group = lax.axis_index("y")
    slot = lax.axis_index("t")
    slots = lax.axis_size("t")
    up = [(i, i + 1) for i in range(slots - 1)]
    down = [(i + 1, i) for i in range(slots - 1)]
    pairs = [[(3, j), (j, 3)] for j in range(3)]
    spans = lax.dynamic_slice_in_dim(span.reshape(3, NSUB * slots, 2), slot * NSUB, NSUB, 1)
    scal = jnp.concatenate([jnp.stack([group, slot]).astype(jnp.int32), spans.reshape(-1)])

    s_kv, c_kv = jnp.concatenate([sk, sv]), jnp.concatenate([ck, cv])
    own = call(squares_kernel, "squares", 0, [shape(8, F32, TOK)], sq, sk, cq, ck)[0]
    c_in = [None] * 3
    s_a = lax.ppermute(s_kv, "t", down)
    c_in[1] = lax.ppermute(c_kv, "y", pairs[1])
    c_in[0] = lax.ppermute(c_kv, "y", pairs[0])
    s_later, s_a = lax.optimization_barrier((s_kv, s_a))
    s_b = lax.ppermute(s_later, "t", up)
    c_in[2] = lax.ppermute(c_kv, "y", pairs[2])
    sums = call(more_squares_kernel, "more", 0, [shape(16, F32, TOK)], own, c_in[2], s_b, c_in[0], c_in[1], s_a)[0]
    sums = lax.all_gather(sums, "head")

    s_out, s_dq, s_dk, s_dv, part_b, part_a = call(
        self_kernel, "selfatt", 1, [shape(TOK, F32)] + [shape(TOK, F32)] * 3 + [shape(2 * TOK, BF16)] * 2,
        scal, sums, gains, sq, sk, sv, do, s_b, s_a, flops=12 * HEADS * TOK * 3 * TOK * DH,
    )
    att, c_dq, *c_parts = call(
        cross_kernel, "cross", 1, [shape(TOK, BF16), shape(TOK, F32)] + [shape(2 * TOK, BF16)] * 3,
        scal, sums, gains, cq, do, *c_in, s_out, flops=12 * HEADS * TOK * 3 * TOK * DH,
    )
    back_b = lax.ppermute(part_a, "t", up)
    part_later, back_b = lax.optimization_barrier((part_b, back_b))
    c_back = [None] * 3
    for j in (1, 0, 2):
        c_back[j] = lax.ppermute(c_parts[j], "y", pairs[j])
    back_a = lax.ppermute(part_later, "t", down)
    svg, cvg, dks, dkc, inner = call(
        gather_kernel, "gather", 1, [shape(TOK, BF16)] * 2 + [shape(TOK, F32)] * 2 + [shape(8, F32, TOK)],
        scal, gains, sq, sk, cq, ck, s_dq, c_dq, s_dk, s_dv, back_b, c_back[1], c_back[0], c_back[2], back_a,
    )
    inner = lax.all_gather(inner, "head")
    g0, g1, g2, g3 = call(
        final_kernel, "final", 1, [shape(TOK, BF16)] * 4, scal, gains, sums, inner, sq, sk, cq, ck, s_dq, dks, c_dq, dkc
    )
    return att, g0, g1, svg, g2, g3, cvg


def solution(mesh):
    seq = mesh.shape["seq"]
    grid = Mesh(mesh.devices.reshape(4, seq // 4, mesh.shape["head"]), ("y", "t", "head"))
    block = P(("y", "t"), "head")
    return jax.shard_map(
        on_device,
        mesh=grid,
        in_specs=(block,) * 7 + (P(None, None, "head"), P()),
        out_specs=(block,) * 7,
        check_vma=False,
    )
```

```python
import functools

import jax
import jax.numpy as jnp
from jax import lax
from jax.experimental import pallas as pl
from jax.experimental.pallas import tpu as pltpu
from jax.sharding import Mesh, PartitionSpec as P

DH = 128
BLK = 64
WIDTH = 1536
NSUB = 4
HEADS = 3
TOK = 256
COLS = 384
COLUMNS = [slice(h * DH, (h + 1) * DH) for h in range(HEADS)]
EPSILON = 1e-06
SCALE = DH ** (-0.5)
MASKED = -1e30
LOG2E = 1.4426950408889634
F32 = jnp.float32
BF16 = jnp.bfloat16
VMEM = pltpu.VMEM
VSPEC = pl.BlockSpec(memory_space=pltpu.VMEM)
SSPEC = pl.BlockSpec(memory_space=pltpu.SMEM)


def dot(a, b, ca, cb):
    return lax.dot_general(a, b, (((ca,), (cb,)), ((), ())), preferred_element_type=F32)


def row_sums(product):
    folded = product[:, 0:128] + product[:, 128:256] + product[:, 256:384]
    return jnp.sum(jnp.transpose(folded), axis=0, keepdims=True)


def squares_kernel(*refs):
    ins, out = refs[:4], refs[-1]
    out[...] = jnp.zeros(out.shape, F32)
    for i, ref in enumerate(ins):
        wide = ref[0:TOK, :].astype(F32)
        out[i : i + 1, :] = row_sums(wide * wide)


def more_squares_kernel(own, *refs):
    ins, out = refs[:-1], refs[-1]
    out[0:8, :] = own[...]
    out[8:16, :] = jnp.zeros((8, TOK), F32)
    for i, ref in enumerate(ins):
        wide = ref[0:TOK, :].astype(F32)
        row = (8, 4, 6, 7, 5)[i]
        out[row : row + 1, :] = row_sums(wide * wide)


def attend(qs, kns, vs, dos, valid, masks, key_side=3):
    heads, blocks = range(len(qs)), range(len(kns[0]))
    scores = [[dot(kns[h][j], qs[h], 1, 1) for j in blocks] for h in heads]
    if masks is not None:
        scores = [[jnp.where(masks[j], scores[h][j], MASKED) for j in blocks] for h in heads]
    dprobs = [[dot(vs[h][j], dos[h], 1, 1) for j in blocks] for h in heads]
    tops = []
    for h in heads:
        peaks = [jnp.max(scores[h][j], axis=0, keepdims=True) for j in blocks]
        if valid is not None:
            peaks = [peaks[0]] + [jnp.where(ok, peak, MASKED) for ok, peak in zip(valid[1:], peaks[1:])]
        tops.append(functools.reduce(jnp.maximum, peaks))
    if valid is None:
        lifts = [[tops[h]] * len(blocks) for h in heads]
    else:
        lifts = [[tops[h]] + [jnp.where(ok, tops[h], -MASKED) for ok in valid[1:]] for h in heads]
    shifted = [[jnp.exp2((scores[h][j] - lifts[h][j]) * (SCALE * LOG2E)) for j in blocks] for h in heads]
    inverse = [1.0 / sum(jnp.sum(e, axis=0, keepdims=True) for e in shifted[h]) for h in heads]
    probs = [[e * inverse[h] for e in shifted[h]] for h in heads]
    weights = [[p.astype(BF16) for p in probs[h]] for h in heads]
    delta = [sum(jnp.sum(p * d, axis=0, keepdims=True) for p, d in zip(probs[h], dprobs[h])) for h in heads]
    dscores = [
        [(p * (d - delta[h]) * SCALE).astype(BF16) for p, d in zip(probs[h], dprobs[h])] for h in heads
    ]
    results = []
    for h in heads:
        out = sum(dot(w, v, 0, 0) for w, v in zip(weights[h], vs[h]))
        dq = sum(dot(ds, kn, 0, 0) for ds, kn in zip(dscores[h], kns[h]))
        dks = [dot(ds, qs[h], 1, 0) for ds in dscores[h][:key_side]]
        dvs = [dot(w, dos[h], 1, 0) for w in weights[h][:key_side]]
        results.append((out, dq, dks, dvs, (tops[h], inverse[h], delta[h])))
    return results


def over_heads(ref):
    return ref[0] + ref[1] + ref[2] + ref[3]


def inverse_rms(sums_ref):
    return jnp.transpose(lax.rsqrt(over_heads(sums_ref) * (1.0 / WIDTH) + EPSILON))


def normed(raw, inv, gain):
    return (raw.astype(F32) * inv * gain).astype(BF16)


def self_kernel(
    scal, sums, gains, q_ref, k_ref, v_ref, do_ref, x_ref, d_ref,
    out_ref, dq_ref, dk_ref, dv_ref, px_ref, stats,
):
    group, slot = scal[0], scal[1]
    tower = (group == 3).astype(jnp.int32)
    inv = inverse_rms(sums)
    qs, kns, vs, dos = [], [], [], []
    for c in COLUMNS:
        gk = gains[tower, 1:2, c]
        qs.append(normed(q_ref[:, c], inv[:, 0:1], gains[tower, 0:1, c]))
        kns.append(
            [
                normed(k_ref[:, c], inv[:, 1:2], gk),
                normed(x_ref[0:TOK, c], inv[:, 5:6], gk),
                normed(d_ref[0:TOK, c], inv[:, 4:5], gk),
            ]
        )
        vs.append([v_ref[:, c], x_ref[TOK:, c], d_ref[TOK:, c]])
        dos.append(do_ref[:, c])
    has_d = (slot > 0) & (slot < 31)
    results = attend(qs, kns, vs, dos, [True, True, has_d], None, key_side=2)
    stats[...] = jnp.zeros(stats.shape, F32)
    stats[9:10, :] = lax.rsqrt(over_heads(sums)[0:1, :] * (1.0 / WIDTH) + EPSILON)
    for h, (c, (out, dq, dks, dvs, rows)) in enumerate(zip(COLUMNS, results)):
        out_ref[:, c] = out
        dq_ref[:, c] = dq
        dk_ref[:, c] = dks[0]
        dv_ref[:, c] = dvs[0]
        px_ref[0:TOK, c] = dks[1].astype(BF16)
        px_ref[TOK:, c] = dvs[1].astype(BF16)
        for i, row in enumerate(rows):
            stats[3 * i + h : 3 * i + h + 1, :] = row


def key_side(tower, inv_k, gains, k_ref, v_ref, qdo_ref, stats):
    inv_q = jnp.transpose(stats[...])[:, 9:10]
    kns = [normed(k_ref[:, c], inv_k, gains[tower, 1:2, c]) for c in COLUMNS]
    qs = [normed(qdo_ref[0:TOK, c], inv_q, gains[tower, 0:1, c]) for c in COLUMNS]
    dos = [qdo_ref[TOK:, c] for c in COLUMNS]
    scores = [dot(kn, q, 1, 1) for kn, q in zip(kns, qs)]
    dprobs = [dot(v_ref[:, c], do, 1, 1) for c, do in zip(COLUMNS, dos)]
    dks, dvs = [], []
    for h in range(HEADS):
        top, inverse, delta = (stats[3 * i + h : 3 * i + h + 1, :] for i in range(3))
        p = jnp.exp2((scores[h] - top) * (SCALE * LOG2E)) * inverse
        ds = (p * (dprobs[h] - delta) * SCALE).astype(BF16)
        dks.append(dot(ds, qs[h], 1, 0))
        dvs.append(dot(p.astype(BF16), dos[h], 1, 0))
    return jnp.concatenate(dks, axis=1), jnp.concatenate(dvs, axis=1)


def cross_kernel(
    scal, sums, gains, q_ref, do_ref, i0, i1, i2,
    out_ref, dq_ref, p0, p1, p2,
):
    group = scal[0]
    audio = group == 3
    inv = inverse_rms(sums)
    sub_row = lax.broadcasted_iota(jnp.int32, (1, TOK), 1) // BLK
    sub_col = lax.broadcasted_iota(jnp.int32, (TOK, 1), 0) // BLK

    def spread(base, offset, sub):
        value = jnp.zeros(sub.shape, jnp.int32)
        for b in range(NSUB):
            value = jnp.where(sub == b, scal[base + 2 * b + offset], value)
        return value

    @pl.when(audio)
    def _():
        masks = []
        for j in range(3):
            lower = spread(2 + 8 * j, 0, sub_col)
            upper = spread(2 + 8 * j, 1, sub_col)
            masks.append((sub_row >= lower) & (sub_row < upper))
        qs = [normed(q_ref[:, c], inv[:, 2:3], gains[1, 2:3, c]) for c in COLUMNS]
        dos = [do_ref[:, c] for c in COLUMNS]
        kns = [
            [normed(r[0:TOK, c], inv[:, 6 + j : 7 + j], gains[0, 3:4, c]) for j, r in enumerate((i0, i1, i2))]
            for c in COLUMNS
        ]
        vs = [[r[TOK:, c] for r in (i0, i1, i2)] for c in COLUMNS]
        for c, (out, dq, dks, dvs, _) in zip(COLUMNS, attend(qs, kns, vs, dos, None, masks)):
            out_ref[:, c] = out
            dq_ref[:, c] = dq
            for ref, dk, dv in zip((p0, p1, p2), dks, dvs):
                ref[0:TOK, c] = dk.astype(BF16)
                ref[TOK:, c] = dv.astype(BF16)

    @pl.when(jnp.logical_not(audio))
    def _():
        base = 2 + 8 * group
        lower = spread(base, 0, sub_row)
        upper = spread(base, 1, sub_row)
        mask = (sub_col >= lower) & (sub_col < upper)
        first, second = group == 0, group == 1

        def pick(a, b, c):
            return jnp.where(first, a, jnp.where(second, b, c))

        inv_k = pick(inv[:, 6:7], inv[:, 7:8], inv[:, 8:9])
        qs = [normed(q_ref[:, c], inv[:, 2:3], gains[0, 2:3, c]) for c in COLUMNS]
        dos = [do_ref[:, c] for c in COLUMNS]
        kns = [
            [normed(pick(i0[0:TOK, c], i1[0:TOK, c], i2[0:TOK, c]), inv_k, gains[1, 3:4, c])] for c in COLUMNS
        ]
        vs = [[pick(i0[TOK:, c], i1[TOK:, c], i2[TOK:, c])] for c in COLUMNS]
        for c, (out, dq, dks, dvs, _) in zip(COLUMNS, attend(qs, kns, vs, dos, None, [mask])):
            out_ref[:, c] = out
            dq_ref[:, c] = dq
            dk = dks[0].astype(BF16)
            dv = dvs[0].astype(BF16)
            for ref in (p0, p1, p2):
                ref[0:TOK, c] = dk
                ref[TOK:, c] = dv


def gather_kernel(
    scal, sums, gains, sq, sk, sv, cq, ck, sdq, cdq, sdk, sdv, qdo, r1, r0, r2, stats, rx,
    svg, cvg, dks_ref, dkc_ref, inner,
):
    tower = (scal[0] == 3).astype(jnp.int32)
    dkc = r0[0:TOK, :].astype(F32) + r1[0:TOK, :].astype(F32) + r2[0:TOK, :].astype(F32)
    cvg[...] = (r0[TOK:, :].astype(F32) + r1[TOK:, :].astype(F32) + r2[TOK:, :].astype(F32)).astype(BF16)
    dk_d, dv_d = key_side(tower, inverse_rms(sums)[:, 1:2], gains, sk, sv, qdo, stats)
    dks = sdk[...] + dk_d + rx[0:TOK, :].astype(F32)
    svg[...] = (sdv[...] + dv_d + rx[TOK:, :].astype(F32)).astype(BF16)
    dks_ref[...] = dks
    dkc_ref[...] = dkc
    inner[...] = jnp.zeros(inner.shape, F32)
    for i, (x, y) in enumerate(((sq, sdq[...]), (sk, dks), (cq, cdq[...]), (ck, dkc))):
        inner[i : i + 1, :] = row_sums(gains[tower, i : i + 1, :] * y * x[...].astype(F32))


def final_kernel(scal, gains, sums, inner, sq, sk, cq, ck, y0, y1, y2, y3, o0, o1, o2, o3):
    tower = (scal[0] == 3).astype(jnp.int32)
    inv = inverse_rms(sums)
    mean = jnp.transpose(over_heads(inner)) * (1.0 / WIDTH)
    for i, (x, y, o) in enumerate(zip((sq, sk, cq, ck), (y0, y1, y2, y3), (o0, o1, o2, o3))):
        r = inv[:, i : i + 1]
        o[...] = (
            r * gains[tower, i : i + 1, :] * y[...] - x[...].astype(F32) * (r * r * r * mean[:, i : i + 1])
        ).astype(BF16)


def shape(rows, dtype, cols=COLS):
    return jax.ShapeDtypeStruct((rows, cols), dtype)


def call(kernel, name, scalars, outs, *args, flops=0):
    nbytes = sum(a.size * a.dtype.itemsize for a in args) + sum(o.size * o.dtype.itemsize for o in outs)
    return pl.pallas_call(
        kernel,
        name=name,
        out_shape=outs,
        in_specs=[SSPEC] * scalars + [VSPEC] * (len(args) - scalars),
        out_specs=[VSPEC] * len(outs),
        compiler_params=pltpu.CompilerParams(vmem_limit_bytes=40 * 1024 * 1024),
        cost_estimate=pl.CostEstimate(flops=flops, bytes_accessed=nbytes, transcendentals=0),
    )(*args)


def on_device(sq, sk, sv, cq, ck, cv, do, gains, span):
    group = lax.axis_index("y")
    slot = lax.axis_index("t")
    slots = lax.axis_size("t")
    x_pairs = [(i, i ^ 1) for i in range(slots)]
    d_pairs = [(i, i + 1) if i % 2 else (i, i - 1) for i in range(1, slots - 1)]
    pairs = [[(3, j), (j, 3)] for j in range(3)]
    spans = lax.dynamic_slice_in_dim(span.reshape(3, NSUB * slots, 2), slot * NSUB, NSUB, 1)
    scal = jnp.concatenate([jnp.stack([group, slot]).astype(jnp.int32), spans.reshape(-1)])

    s_kv, c_kv = jnp.concatenate([sk, sv]), jnp.concatenate([ck, cv])
    scal, sq = lax.optimization_barrier((scal, sq))
    own = call(squares_kernel, "squares", 0, [shape(8, F32, TOK)], sq, sk, cq, ck, do, sv, gains)[0]
    c_in = [None] * 3
    s_x = lax.ppermute(s_kv, "t", x_pairs)
    c_in[1] = lax.ppermute(c_kv, "y", pairs[1])
    c_in[0] = lax.ppermute(c_kv, "y", pairs[0])
    s_later, s_x = lax.optimization_barrier((s_kv, s_x))
    s_d = lax.ppermute(s_later, "t", d_pairs)
    c_in[2] = lax.ppermute(c_kv, "y", pairs[2])
    qdo, own = lax.optimization_barrier((jnp.concatenate([sq, do]), own))
    sums = call(
        more_squares_kernel, "more", 0, [shape(16, F32, TOK)], own, c_in[2], s_d, c_in[0], c_in[1], s_x
    )[0]
    sums = lax.all_gather(sums, "head")

    qdo, sums = lax.optimization_barrier((qdo, sums))
    d_qdo = lax.ppermute(qdo, "t", d_pairs)
    c_out, c_dq, *c_parts = call(
        cross_kernel, "cross", 1, [shape(TOK, F32)] * 2 + [shape(2 * TOK, BF16)] * 3,
        scal, sums, gains, cq, do, *c_in, flops=12 * HEADS * TOK * 3 * TOK * DH,
    )
    c_back = [None] * 3
    for j in (1, 0, 2):
        c_back[j] = lax.ppermute(c_parts[j], "y", pairs[j])
    sq_later, d_qdo, c_out = lax.optimization_barrier((sq, d_qdo, c_out))
    s_out, s_dq, s_dk, s_dv, part_x, stats = call(
        self_kernel, "selfatt", 1, [shape(TOK, F32)] * 4 + [shape(2 * TOK, BF16), shape(16, F32, TOK)],
        scal, sums, gains, sq_later, sk, sv, do, s_x, s_d, flops=12 * HEADS * TOK * 3 * TOK * DH,
    )
    d_stats = lax.ppermute(stats, "t", d_pairs)
    back_x = lax.ppermute(part_x, "t", x_pairs)
    att = (s_out + c_out).astype(BF16)
    svg, cvg, dks, dkc, inner = call(
        gather_kernel, "gather", 1, [shape(TOK, BF16)] * 2 + [shape(TOK, F32)] * 2 + [shape(8, F32, TOK)],
        scal, sums, gains, sq, sk, sv, cq, ck, s_dq, c_dq, s_dk, s_dv, d_qdo, c_back[1], c_back[0], c_back[2], d_stats, back_x,
        flops=8 * HEADS * TOK * TOK * DH,
    )
    inner = lax.all_gather(inner, "head")
    g0, g1, g2, g3 = call(
        final_kernel, "final", 1, [shape(TOK, BF16)] * 4, scal, gains, sums, inner, sq, sk, cq, ck, s_dq, dks, c_dq, dkc
    )
    return att, g0, g1, svg, g2, g3, cvg


def solution(mesh):
    seq = mesh.shape["seq"]
    grid = Mesh(mesh.devices.reshape(4, seq // 4, mesh.shape["head"]), ("y", "t", "head"))
    block = P(("y", "t"), "head")
    return jax.shard_map(
        on_device,
        mesh=grid,
        in_specs=(block,) * 7 + (P(None, None, "head"), P()),
        out_specs=(block,) * 7,
        check_vma=False,
    )
```

```python
import functools

import jax
import jax.numpy as jnp
from jax import lax
from jax.experimental import pallas as pl
from jax.experimental.pallas import tpu as pltpu
from jax.sharding import Mesh, PartitionSpec as P

DH = 128
BLK = 64
WIDTH = 1536
NSUB = 4
HEADS = 3
TOK = 256
COLS = 384
COLUMNS = [slice(h * DH, (h + 1) * DH) for h in range(HEADS)]
EPSILON = 1e-06
SCALE = DH ** (-0.5)
MASKED = -1e30
LOG2E = 1.4426950408889634
F32 = jnp.float32
BF16 = jnp.bfloat16
VMEM = pltpu.VMEM
VSPEC = pl.BlockSpec(memory_space=pltpu.VMEM)
SSPEC = pl.BlockSpec(memory_space=pltpu.SMEM)


def dot(a, b, ca, cb):
    return lax.dot_general(a, b, (((ca,), (cb,)), ((), ())), preferred_element_type=F32)


def row_sums(product):
    folded = product[:, 0:128] + product[:, 128:256] + product[:, 256:384]
    return jnp.sum(jnp.transpose(folded), axis=0, keepdims=True)


def squares_kernel(*refs):
    ins, out = refs[:4], refs[-1]
    out[...] = jnp.zeros(out.shape, F32)
    for i, ref in enumerate(ins):
        wide = ref[0:TOK, :].astype(F32)
        out[i : i + 1, :] = row_sums(wide * wide)


def more_squares_kernel(own, *refs):
    ins, out = refs[:-1], refs[-1]
    out[0:8, :] = own[...]
    out[8:16, :] = jnp.zeros((8, TOK), F32)
    for i, ref in enumerate(ins):
        wide = ref[0:TOK, :].astype(F32)
        row = (8, 4, 7, 6, 5)[i]
        out[row : row + 1, :] = row_sums(wide * wide)


def attend(qs, kns, vs, dos, valid, masks, key_side=3):
    heads, blocks = range(len(qs)), range(len(kns[0]))
    scores = [[dot(kns[h][j], qs[h], 1, 1) for j in blocks] for h in heads]
    if masks is not None:
        scores = [[jnp.where(masks[j], scores[h][j], MASKED) for j in blocks] for h in heads]
    dprobs = [[dot(vs[h][j], dos[h], 1, 1) for j in blocks] for h in heads]
    tops = []
    for h in heads:
        peaks = [jnp.max(scores[h][j], axis=0, keepdims=True) for j in blocks]
        if valid is not None:
            peaks = [peaks[0]] + [jnp.where(ok, peak, MASKED) for ok, peak in zip(valid[1:], peaks[1:])]
        tops.append(functools.reduce(jnp.maximum, peaks))
    if valid is None:
        lifts = [[tops[h]] * len(blocks) for h in heads]
    else:
        lifts = [[tops[h]] + [jnp.where(ok, tops[h], -MASKED) for ok in valid[1:]] for h in heads]
    shifted = [[jnp.exp2((scores[h][j] - lifts[h][j]) * (SCALE * LOG2E)) for j in blocks] for h in heads]
    inverse = [1.0 / sum(jnp.sum(e, axis=0, keepdims=True) for e in shifted[h]) for h in heads]
    probs = [[e * inverse[h] for e in shifted[h]] for h in heads]
    weights = [[p.astype(BF16) for p in probs[h]] for h in heads]
    delta = [sum(jnp.sum(p * d, axis=0, keepdims=True) for p, d in zip(probs[h], dprobs[h])) for h in heads]
    dscores = [
        [(p * (d - delta[h]) * SCALE).astype(BF16) for p, d in zip(probs[h], dprobs[h])] for h in heads
    ]
    results = []
    for h in heads:
        out = sum(dot(w, v, 0, 0) for w, v in zip(weights[h], vs[h]))
        dq = sum(dot(ds, kn, 0, 0) for ds, kn in zip(dscores[h], kns[h]))
        dks = [dot(ds, qs[h], 1, 0) for ds in dscores[h][:key_side]]
        dvs = [dot(w, dos[h], 1, 0) for w in weights[h][:key_side]]
        results.append((out, dq, dks, dvs, (tops[h], inverse[h], delta[h])))
    return results


def over_heads(ref):
    return ref[0] + ref[1] + ref[2] + ref[3]


def inverse_rms(sums_ref):
    return jnp.transpose(lax.rsqrt(over_heads(sums_ref) * (1.0 / WIDTH) + EPSILON))


def normed(raw, inv, gain):
    return (raw.astype(F32) * inv * gain).astype(BF16)


def self_kernel(
    scal, sums, gains, q_ref, k_ref, v_ref, do_ref, x_ref, d_ref,
    out_ref, dq_ref, dk_ref, dv_ref, px_ref, stats,
):
    group, slot = scal[0], scal[1]
    tower = (group == 3).astype(jnp.int32)
    inv = inverse_rms(sums)
    qs, kns, vs, dos = [], [], [], []
    for c in COLUMNS:
        gk = gains[tower, 1:2, c]
        qs.append(normed(q_ref[:, c], inv[:, 0:1], gains[tower, 0:1, c]))
        kns.append(
            [
                normed(k_ref[:, c], inv[:, 1:2], gk),
                normed(x_ref[0:TOK, c], inv[:, 5:6], gk),
                normed(d_ref[0:TOK, c], inv[:, 4:5], gk),
            ]
        )
        vs.append([v_ref[:, c], x_ref[TOK:, c], d_ref[TOK:, c]])
        dos.append(do_ref[:, c])
    has_d = (slot > 0) & (slot < 31)
    results = attend(qs, kns, vs, dos, [True, True, has_d], None, key_side=2)
    stats[...] = jnp.zeros(stats.shape, F32)
    stats[9:10, :] = lax.rsqrt(over_heads(sums)[0:1, :] * (1.0 / WIDTH) + EPSILON)
    for h, (c, (out, dq, dks, dvs, rows)) in enumerate(zip(COLUMNS, results)):
        out_ref[:, c] = out
        dq_ref[:, c] = dq
        dk_ref[:, c] = dks[0]
        dv_ref[:, c] = dvs[0]
        px_ref[0:TOK, c] = dks[1].astype(BF16)
        px_ref[TOK:, c] = dvs[1].astype(BF16)
        for i, row in enumerate(rows):
            stats[3 * i + h : 3 * i + h + 1, :] = row


def key_side_kernel(scal, sums, gains, k_ref, v_ref, qdo_ref, stats, dk_in, dv_in, dk_ref, dv_ref):
    tower = (scal[0] == 3).astype(jnp.int32)
    inv_k = inverse_rms(sums)[:, 1:2]
    inv_q = jnp.transpose(stats[...])[:, 9:10]
    kns = [normed(k_ref[:, c], inv_k, gains[tower, 1:2, c]) for c in COLUMNS]
    qs = [normed(qdo_ref[0:TOK, c], inv_q, gains[tower, 0:1, c]) for c in COLUMNS]
    dos = [qdo_ref[TOK:, c] for c in COLUMNS]
    scores = [dot(kn, q, 1, 1) for kn, q in zip(kns, qs)]
    dprobs = [dot(v_ref[:, c], do, 1, 1) for c, do in zip(COLUMNS, dos)]
    for h, c in enumerate(COLUMNS):
        top, inverse, delta = (stats[3 * i + h : 3 * i + h + 1, :] for i in range(3))
        p = jnp.exp2((scores[h] - top) * (SCALE * LOG2E)) * inverse
        ds = (p * (dprobs[h] - delta) * SCALE).astype(BF16)
        dk_ref[:, c] = dk_in[:, c] + dot(ds, qs[h], 1, 0)
        dv_ref[:, c] = dv_in[:, c] + dot(p.astype(BF16), dos[h], 1, 0)


def cross_kernel(
    scal, sums, gains, q_ref, do_ref, i0, i1, i2,
    out_ref, dq_ref, p0, p1, p2,
):
    group = scal[0]
    audio = group == 3
    inv = inverse_rms(sums)
    sub_row = lax.broadcasted_iota(jnp.int32, (1, TOK), 1) // BLK
    sub_col = lax.broadcasted_iota(jnp.int32, (TOK, 1), 0) // BLK

    def spread(base, offset, sub):
        value = jnp.zeros(sub.shape, jnp.int32)
        for b in range(NSUB):
            value = jnp.where(sub == b, scal[base + 2 * b + offset], value)
        return value

    @pl.when(audio)
    def _():
        masks = []
        for j in range(3):
            lower = spread(2 + 8 * j, 0, sub_col)
            upper = spread(2 + 8 * j, 1, sub_col)
            masks.append((sub_row >= lower) & (sub_row < upper))
        qs = [normed(q_ref[:, c], inv[:, 2:3], gains[1, 2:3, c]) for c in COLUMNS]
        dos = [do_ref[:, c] for c in COLUMNS]
        kns = [
            [normed(r[0:TOK, c], inv[:, 6 + j : 7 + j], gains[0, 3:4, c]) for j, r in enumerate((i0, i1, i2))]
            for c in COLUMNS
        ]
        vs = [[r[TOK:, c] for r in (i0, i1, i2)] for c in COLUMNS]
        for c, (out, dq, dks, dvs, _) in zip(COLUMNS, attend(qs, kns, vs, dos, None, masks)):
            out_ref[:, c] = out
            dq_ref[:, c] = dq
            for ref, dk, dv in zip((p0, p1, p2), dks, dvs):
                ref[0:TOK, c] = dk.astype(BF16)
                ref[TOK:, c] = dv.astype(BF16)

    @pl.when(jnp.logical_not(audio))
    def _():
        base = 2 + 8 * group
        lower = spread(base, 0, sub_row)
        upper = spread(base, 1, sub_row)
        mask = (sub_col >= lower) & (sub_col < upper)
        first, second = group == 0, group == 1

        def pick(a, b, c):
            return jnp.where(first, a, jnp.where(second, b, c))

        inv_k = pick(inv[:, 6:7], inv[:, 7:8], inv[:, 8:9])
        qs = [normed(q_ref[:, c], inv[:, 2:3], gains[0, 2:3, c]) for c in COLUMNS]
        dos = [do_ref[:, c] for c in COLUMNS]
        kns = [
            [normed(pick(i0[0:TOK, c], i1[0:TOK, c], i2[0:TOK, c]), inv_k, gains[1, 3:4, c])] for c in COLUMNS
        ]
        vs = [[pick(i0[TOK:, c], i1[TOK:, c], i2[TOK:, c])] for c in COLUMNS]
        for c, (out, dq, dks, dvs, _) in zip(COLUMNS, attend(qs, kns, vs, dos, None, [mask])):
            out_ref[:, c] = out
            dq_ref[:, c] = dq
            dk = dks[0].astype(BF16)
            dv = dvs[0].astype(BF16)
            for ref in (p0, p1, p2):
                ref[0:TOK, c] = dk
                ref[TOK:, c] = dv


def gather_kernel(
    scal, gains, sq, sk, cq, ck, sdq, cdq, sdk, sdv, r0, r1, r2, rx,
    svg, cvg, dks_ref, dkc_ref, inner,
):
    tower = (scal[0] == 3).astype(jnp.int32)
    dkc = r0[0:TOK, :].astype(F32) + r1[0:TOK, :].astype(F32) + r2[0:TOK, :].astype(F32)
    cvg[...] = (r0[TOK:, :].astype(F32) + r1[TOK:, :].astype(F32) + r2[TOK:, :].astype(F32)).astype(BF16)
    dks = sdk[...] + rx[0:TOK, :].astype(F32)
    svg[...] = (sdv[...] + rx[TOK:, :].astype(F32)).astype(BF16)
    dks_ref[...] = dks
    dkc_ref[...] = dkc
    inner[...] = jnp.zeros(inner.shape, F32)
    for i, (x, y) in enumerate(((sq, sdq[...]), (sk, dks), (cq, cdq[...]), (ck, dkc))):
        inner[i : i + 1, :] = row_sums(gains[tower, i : i + 1, :] * y * x[...].astype(F32))


def final_kernel(scal, gains, sums, inner, sq, sk, cq, ck, y0, y1, y2, y3, o0, o1, o2, o3):
    tower = (scal[0] == 3).astype(jnp.int32)
    inv = inverse_rms(sums)
    mean = jnp.transpose(over_heads(inner)) * (1.0 / WIDTH)
    for i, (x, y, o) in enumerate(zip((sq, sk, cq, ck), (y0, y1, y2, y3), (o0, o1, o2, o3))):
        r = inv[:, i : i + 1]
        o[...] = (
            r * gains[tower, i : i + 1, :] * y[...] - x[...].astype(F32) * (r * r * r * mean[:, i : i + 1])
        ).astype(BF16)


def shape(rows, dtype, cols=COLS):
    return jax.ShapeDtypeStruct((rows, cols), dtype)


def call(kernel, name, scalars, outs, *args, flops=0):
    nbytes = sum(a.size * a.dtype.itemsize for a in args) + sum(o.size * o.dtype.itemsize for o in outs)
    return pl.pallas_call(
        kernel,
        name=name,
        out_shape=outs,
        in_specs=[SSPEC] * scalars + [VSPEC] * (len(args) - scalars),
        out_specs=[VSPEC] * len(outs),
        compiler_params=pltpu.CompilerParams(vmem_limit_bytes=40 * 1024 * 1024),
        cost_estimate=pl.CostEstimate(flops=flops, bytes_accessed=nbytes, transcendentals=0),
    )(*args)


def on_device(sq, sk, sv, cq, ck, cv, do, gains, span):
    group = lax.axis_index("y")
    slot = lax.axis_index("t")
    slots = lax.axis_size("t")
    x_pairs = [(i, i ^ 1) for i in range(slots)]
    d_pairs = [(i, i + 1) if i % 2 else (i, i - 1) for i in range(1, slots - 1)]
    pairs = [[(3, j), (j, 3)] for j in range(3)]
    spans = lax.dynamic_slice_in_dim(span.reshape(3, NSUB * slots, 2), slot * NSUB, NSUB, 1)
    scal = jnp.concatenate([jnp.stack([group, slot]).astype(jnp.int32), spans.reshape(-1)])

    s_kv, c_kv = jnp.concatenate([sk, sv]), jnp.concatenate([ck, cv])
    scal, sq = lax.optimization_barrier((scal, sq))
    own = call(squares_kernel, "squares", 0, [shape(8, F32, TOK)], sq, sk, cq, ck, do, sv, gains)[0]
    c_in = [None] * 3
    s_x = lax.ppermute(s_kv, "t", x_pairs)
    c_in[1] = lax.ppermute(c_kv, "y", pairs[1])
    c_in[0] = lax.ppermute(c_kv, "y", pairs[0])
    s_later, s_x = lax.optimization_barrier((s_kv, s_x))
    s_d = lax.ppermute(s_later, "t", d_pairs)
    c_in[2] = lax.ppermute(c_kv, "y", pairs[2])
    qdo, own = lax.optimization_barrier((jnp.concatenate([sq, do]), own))
    sums = call(
        more_squares_kernel, "more", 0, [shape(16, F32, TOK)], own, c_in[2], s_d, c_in[1], c_in[0], s_x
    )[0]
    sums = lax.all_gather(sums, "head")

    qdo, sums = lax.optimization_barrier((qdo, sums))
    d_qdo = lax.ppermute(qdo, "t", d_pairs)
    c_out, c_dq, *c_parts = call(
        cross_kernel, "cross", 1, [shape(TOK, F32)] * 2 + [shape(2 * TOK, BF16)] * 3,
        scal, sums, gains, cq, do, *c_in, flops=12 * HEADS * TOK * 3 * TOK * DH,
    )
    c_back = [None] * 3
    for j in (1, 0, 2):
        c_back[j] = lax.ppermute(c_parts[j], "y", pairs[j])
    sq_later, d_qdo, c_out = lax.optimization_barrier((sq, d_qdo, c_out))
    s_out, s_dq, s_dk, s_dv, part_x, stats = call(
        self_kernel, "selfatt", 1, [shape(TOK, F32)] * 4 + [shape(2 * TOK, BF16), shape(16, F32, TOK)],
        scal, sums, gains, sq_later, sk, sv, do, s_x, s_d, flops=12 * HEADS * TOK * 3 * TOK * DH,
    )
    d_stats = lax.ppermute(stats, "t", d_pairs)
    back_x = lax.ppermute(part_x, "t", x_pairs)
    s_dk, s_dv = call(
        key_side_kernel, "keyside", 1, [shape(TOK, F32)] * 2,
        scal, sums, gains, sk, sv, d_qdo, d_stats, s_dk, s_dv, flops=8 * HEADS * TOK * TOK * DH,
    )
    att = (s_out + c_out).astype(BF16)
    svg, cvg, dks, dkc, inner = call(
        gather_kernel, "gather", 1, [shape(TOK, BF16)] * 2 + [shape(TOK, F32)] * 2 + [shape(8, F32, TOK)],
        scal, gains, sq, sk, cq, ck, s_dq, c_dq, s_dk, s_dv, c_back[0], c_back[1], c_back[2], back_x,
    )
    inner = lax.all_gather(inner, "head")
    g0, g1, g2, g3 = call(
        final_kernel, "final", 1, [shape(TOK, BF16)] * 4, scal, gains, sums, inner, sq, sk, cq, ck, s_dq, dks, c_dq, dkc
    )
    return att, g0, g1, svg, g2, g3, cvg


def solution(mesh):
    seq = mesh.shape["seq"]
    grid = Mesh(mesh.devices.reshape(4, seq // 4, mesh.shape["head"]), ("y", "t", "head"))
    block = P(("y", "t"), "head")
    return jax.shard_map(
        on_device,
        mesh=grid,
        in_specs=(block,) * 7 + (P(None, None, "head"), P()),
        out_specs=(block,) * 7,
        check_vma=False,
    )
```

```python
import functools

import jax
import jax.numpy as jnp
from jax import lax
from jax.experimental import pallas as pl
from jax.experimental.pallas import tpu as pltpu
from jax.sharding import Mesh, PartitionSpec as P

DH = 128
BLK = 64
WIDTH = 1536
NSUB = 4
HEADS = 3
TOK = 256
COLS = 384
COLUMNS = [slice(h * DH, (h + 1) * DH) for h in range(HEADS)]
EPSILON = 1e-06
SCALE = DH ** (-0.5)
MASKED = -1e30
LOG2E = 1.4426950408889634
F32 = jnp.float32
BF16 = jnp.bfloat16
VMEM = pltpu.VMEM
VSPEC = pl.BlockSpec(memory_space=pltpu.VMEM)
SSPEC = pl.BlockSpec(memory_space=pltpu.SMEM)


def dot(a, b, ca, cb):
    return lax.dot_general(a, b, (((ca,), (cb,)), ((), ())), preferred_element_type=F32)


def row_sums(product):
    folded = product[:, 0:128] + product[:, 128:256] + product[:, 256:384]
    return jnp.sum(jnp.transpose(folded), axis=0, keepdims=True)


def squares_kernel(*refs):
    ins, out = refs[:4], refs[-1]
    out[...] = jnp.zeros(out.shape, F32)
    for i, ref in enumerate(ins):
        wide = ref[0:TOK, :].astype(F32)
        out[i : i + 1, :] = row_sums(wide * wide)


def more_squares_kernel(own, *refs):
    ins, out = refs[:-1], refs[-1]
    out[0:8, :] = own[...]
    out[8:16, :] = jnp.zeros((8, TOK), F32)
    for i, ref in enumerate(ins):
        wide = ref[0:TOK, :].astype(F32)
        row = (8, 4, 7, 6, 5)[i]
        out[row : row + 1, :] = row_sums(wide * wide)


def attend(qs, kns, vs, dos, valid, masks, key_side=3):
    heads, blocks = range(len(qs)), range(len(kns[0]))
    scores = [[dot(kns[h][j], qs[h], 1, 1) for j in blocks] for h in heads]
    if masks is not None:
        scores = [[jnp.where(masks[j], scores[h][j], MASKED) for j in blocks] for h in heads]
    dprobs = [[dot(vs[h][j], dos[h], 1, 1) for j in blocks] for h in heads]
    tops = []
    for h in heads:
        peaks = [jnp.max(scores[h][j], axis=0, keepdims=True) for j in blocks]
        if valid is not None:
            peaks = [peaks[0]] + [jnp.where(ok, peak, MASKED) for ok, peak in zip(valid[1:], peaks[1:])]
        tops.append(functools.reduce(jnp.maximum, peaks))
    if valid is None:
        lifts = [[tops[h]] * len(blocks) for h in heads]
    else:
        lifts = [[tops[h]] + [jnp.where(ok, tops[h], -MASKED) for ok in valid[1:]] for h in heads]
    shifted = [[jnp.exp2((scores[h][j] - lifts[h][j]) * (SCALE * LOG2E)) for j in blocks] for h in heads]
    inverse = [1.0 / sum(jnp.sum(e, axis=0, keepdims=True) for e in shifted[h]) for h in heads]
    probs = [[e * inverse[h] for e in shifted[h]] for h in heads]
    weights = [[p.astype(BF16) for p in probs[h]] for h in heads]
    delta = [sum(jnp.sum(p * d, axis=0, keepdims=True) for p, d in zip(probs[h], dprobs[h])) for h in heads]
    dscores = [
        [(p * (d - delta[h]) * SCALE).astype(BF16) for p, d in zip(probs[h], dprobs[h])] for h in heads
    ]
    results = []
    for h in heads:
        out = sum(dot(w, v, 0, 0) for w, v in zip(weights[h], vs[h]))
        dq = sum(dot(ds, kn, 0, 0) for ds, kn in zip(dscores[h], kns[h]))
        dks = [dot(ds, qs[h], 1, 0) for ds in dscores[h][:key_side]]
        dvs = [dot(w, dos[h], 1, 0) for w in weights[h][:key_side]]
        results.append((out, dq, dks, dvs, (tops[h], inverse[h], delta[h])))
    return results


def over_heads(ref):
    return ref[0] + ref[1] + ref[2] + ref[3]


def inverse_rms(sums_ref):
    return jnp.transpose(lax.rsqrt(over_heads(sums_ref) * (1.0 / WIDTH) + EPSILON))


def normed(raw, inv, gain):
    return (raw.astype(F32) * inv * gain).astype(BF16)


def self_kernel(
    scal, sums, gains, q_ref, k_ref, v_ref, do_ref, x_ref, d_ref,
    out_ref, dq_ref, dk_ref, dv_ref, px_ref, stats,
):
    group, slot = scal[0], scal[1]
    tower = (group == 3).astype(jnp.int32)
    inv = inverse_rms(sums)
    qs, kns, vs, dos = [], [], [], []
    for c in COLUMNS:
        gk = gains[tower, 1:2, c]
        qs.append(normed(q_ref[:, c], inv[:, 0:1], gains[tower, 0:1, c]))
        kns.append(
            [
                normed(k_ref[:, c], inv[:, 1:2], gk),
                normed(x_ref[0:TOK, c], inv[:, 5:6], gk),
                normed(d_ref[0:TOK, c], inv[:, 4:5], gk),
            ]
        )
        vs.append([v_ref[:, c], x_ref[TOK:, c], d_ref[TOK:, c]])
        dos.append(do_ref[:, c])
    has_d = (slot > 0) & (slot < 31)
    results = attend(qs, kns, vs, dos, [True, True, has_d], None, key_side=2)
    stats[...] = jnp.zeros(stats.shape, F32)
    stats[9:10, :] = lax.rsqrt(over_heads(sums)[0:1, :] * (1.0 / WIDTH) + EPSILON)
    for h, (c, (out, dq, dks, dvs, rows)) in enumerate(zip(COLUMNS, results)):
        out_ref[:, c] = out
        dq_ref[:, c] = dq
        dk_ref[:, c] = dks[0]
        dv_ref[:, c] = dvs[0]
        px_ref[0:TOK, c] = dks[1].astype(BF16)
        px_ref[TOK:, c] = dvs[1].astype(BF16)
        for i, row in enumerate(rows):
            stats[3 * i + h : 3 * i + h + 1, :] = row


def key_side_kernel(scal, sums, gains, k_ref, v_ref, qdo_ref, stats, dk_in, dv_in, dk_ref, dv_ref):
    tower = (scal[0] == 3).astype(jnp.int32)
    inv_k = inverse_rms(sums)[:, 1:2]
    inv_q = jnp.transpose(stats[...])[:, 9:10]
    kns = [normed(k_ref[:, c], inv_k, gains[tower, 1:2, c]) for c in COLUMNS]
    qs = [normed(qdo_ref[0:TOK, c], inv_q, gains[tower, 0:1, c]) for c in COLUMNS]
    dos = [qdo_ref[TOK:, c] for c in COLUMNS]
    scores = [dot(kn, q, 1, 1) for kn, q in zip(kns, qs)]
    dprobs = [dot(v_ref[:, c], do, 1, 1) for c, do in zip(COLUMNS, dos)]
    for h, c in enumerate(COLUMNS):
        top, inverse, delta = (stats[3 * i + h : 3 * i + h + 1, :] for i in range(3))
        p = jnp.exp2((scores[h] - top) * (SCALE * LOG2E)) * inverse
        ds = (p * (dprobs[h] - delta) * SCALE).astype(BF16)
        dk_ref[:, c] = dk_in[:, c] + dot(ds, qs[h], 1, 0)
        dv_ref[:, c] = dv_in[:, c] + dot(p.astype(BF16), dos[h], 1, 0)


def cross_kernel(
    scal, sums, gains, q_ref, do_ref, i0, i1, i2,
    out_ref, dq_ref, p0, p1, p2,
):
    group = scal[0]
    audio = group == 3
    inv = inverse_rms(sums)
    sub_row = lax.broadcasted_iota(jnp.int32, (1, TOK), 1) // BLK
    sub_col = lax.broadcasted_iota(jnp.int32, (TOK, 1), 0) // BLK

    def spread(base, offset, sub):
        value = jnp.zeros(sub.shape, jnp.int32)
        for b in range(NSUB):
            value = jnp.where(sub == b, scal[base + 2 * b + offset], value)
        return value

    @pl.when(audio)
    def _():
        masks = []
        for j in range(3):
            lower = spread(2 + 8 * j, 0, sub_col)
            upper = spread(2 + 8 * j, 1, sub_col)
            masks.append((sub_row >= lower) & (sub_row < upper))
        qs = [normed(q_ref[:, c], inv[:, 2:3], gains[1, 2:3, c]) for c in COLUMNS]
        dos = [do_ref[:, c] for c in COLUMNS]
        kns = [
            [normed(r[0:TOK, c], inv[:, 6 + j : 7 + j], gains[0, 3:4, c]) for j, r in enumerate((i0, i1, i2))]
            for c in COLUMNS
        ]
        vs = [[r[TOK:, c] for r in (i0, i1, i2)] for c in COLUMNS]
        for c, (out, dq, dks, dvs, _) in zip(COLUMNS, attend(qs, kns, vs, dos, None, masks)):
            out_ref[:, c] = out
            dq_ref[:, c] = dq
            for ref, dk, dv in zip((p0, p1, p2), dks, dvs):
                ref[0:TOK, c] = dk.astype(BF16)
                ref[TOK:, c] = dv.astype(BF16)

    @pl.when(jnp.logical_not(audio))
    def _():
        base = 2 + 8 * group
        lower = spread(base, 0, sub_row)
        upper = spread(base, 1, sub_row)
        mask = (sub_col >= lower) & (sub_col < upper)
        first, second = group == 0, group == 1

        def pick(a, b, c):
            return jnp.where(first, a, jnp.where(second, b, c))

        inv_k = pick(inv[:, 6:7], inv[:, 7:8], inv[:, 8:9])
        qs = [normed(q_ref[:, c], inv[:, 2:3], gains[0, 2:3, c]) for c in COLUMNS]
        dos = [do_ref[:, c] for c in COLUMNS]
        kns = [
            [normed(pick(i0[0:TOK, c], i1[0:TOK, c], i2[0:TOK, c]), inv_k, gains[1, 3:4, c])] for c in COLUMNS
        ]
        vs = [[pick(i0[TOK:, c], i1[TOK:, c], i2[TOK:, c])] for c in COLUMNS]
        for c, (out, dq, dks, dvs, _) in zip(COLUMNS, attend(qs, kns, vs, dos, None, [mask])):
            out_ref[:, c] = out
            dq_ref[:, c] = dq
            dk = dks[0].astype(BF16)
            dv = dvs[0].astype(BF16)
            for ref in (p0, p1, p2):
                ref[0:TOK, c] = dk
                ref[TOK:, c] = dv


def gather_kernel(
    scal, gains, sq, sk, cq, ck, sdq, cdq, sdk, sdv, r0, r1, r2, rx,
    svg, cvg, dks_ref, dkc_ref, inner,
):
    tower = (scal[0] == 3).astype(jnp.int32)
    dkc = r0[0:TOK, :].astype(F32) + r1[0:TOK, :].astype(F32) + r2[0:TOK, :].astype(F32)
    cvg[...] = (r0[TOK:, :].astype(F32) + r1[TOK:, :].astype(F32) + r2[TOK:, :].astype(F32)).astype(BF16)
    dks = sdk[...] + rx[0:TOK, :].astype(F32)
    svg[...] = (sdv[...] + rx[TOK:, :].astype(F32)).astype(BF16)
    dks_ref[...] = dks
    dkc_ref[...] = dkc
    inner[...] = jnp.zeros(inner.shape, F32)
    for i, (x, y) in enumerate(((sq, sdq[...]), (sk, dks), (cq, cdq[...]), (ck, dkc))):
        inner[i : i + 1, :] = row_sums(gains[tower, i : i + 1, :] * y * x[...].astype(F32))


def final_kernel(scal, gains, sums, inner, sq, sk, cq, ck, y0, y1, y2, y3, o0, o1, o2, o3):
    tower = (scal[0] == 3).astype(jnp.int32)
    inv = inverse_rms(sums)
    mean = jnp.transpose(over_heads(inner)) * (1.0 / WIDTH)
    for i, (x, y, o) in enumerate(zip((sq, sk, cq, ck), (y0, y1, y2, y3), (o0, o1, o2, o3))):
        r = inv[:, i : i + 1]
        o[...] = (
            r * gains[tower, i : i + 1, :] * y[...] - x[...].astype(F32) * (r * r * r * mean[:, i : i + 1])
        ).astype(BF16)


def shape(rows, dtype, cols=COLS):
    return jax.ShapeDtypeStruct((rows, cols), dtype)


def call(kernel, name, scalars, outs, *args, flops=0):
    nbytes = sum(a.size * a.dtype.itemsize for a in args) + sum(o.size * o.dtype.itemsize for o in outs)
    return pl.pallas_call(
        kernel,
        name=name,
        out_shape=outs,
        in_specs=[SSPEC] * scalars + [VSPEC] * (len(args) - scalars),
        out_specs=[VSPEC] * len(outs),
        compiler_params=pltpu.CompilerParams(vmem_limit_bytes=40 * 1024 * 1024),
        cost_estimate=pl.CostEstimate(flops=flops, bytes_accessed=nbytes, transcendentals=0),
    )(*args)


def on_device(sq, sk, sv, cq, ck, cv, do, gains, span):
    group = lax.axis_index("y")
    slot = lax.axis_index("t")
    slots = lax.axis_size("t")
    x_pairs = [(i, i ^ 1) for i in range(slots)]
    d_pairs = [(i, i + 1) if i % 2 else (i, i - 1) for i in range(1, slots - 1)]
    pairs = [[(3, j), (j, 3)] for j in range(3)]
    spans = lax.dynamic_slice_in_dim(span.reshape(3, NSUB * slots, 2), slot * NSUB, NSUB, 1)
    scal = jnp.concatenate([jnp.stack([group, slot]).astype(jnp.int32), spans.reshape(-1)])

    s_kv, c_kv = jnp.concatenate([sk, sv]), jnp.concatenate([ck, cv])
    scal, sq = lax.optimization_barrier((scal, sq))
    own = call(squares_kernel, "squares", 0, [shape(8, F32, TOK)], sq, sk, cq, ck, do, sv, gains)[0]
    c_in = [None] * 3
    s_x = lax.ppermute(s_kv, "t", x_pairs)
    c_in[1] = lax.ppermute(c_kv, "y", pairs[1])
    c_in[0] = lax.ppermute(c_kv, "y", pairs[0])
    s_later, s_x = lax.optimization_barrier((s_kv, s_x))
    s_d = lax.ppermute(s_later, "t", d_pairs)
    c_in[2] = lax.ppermute(c_kv, "y", pairs[2])
    qdo, own = lax.optimization_barrier((jnp.concatenate([sq, do]), own))
    sums = call(
        more_squares_kernel, "more", 0, [shape(16, F32, TOK)], own, c_in[2], s_d, c_in[1], c_in[0], s_x
    )[0]
    sums = lax.all_gather(sums, "head")

    c_out, c_dq, *c_parts = call(
        cross_kernel, "cross", 1, [shape(TOK, F32)] * 2 + [shape(2 * TOK, BF16)] * 3,
        scal, sums, gains, cq, do, *c_in, flops=12 * HEADS * TOK * 3 * TOK * DH,
    )
    c_back = [None] * 3
    for j in (1, 0, 2):
        c_back[j] = lax.ppermute(c_parts[j], "y", pairs[j])
    sq_later, qdo, c_out = lax.optimization_barrier((sq, qdo, c_out))
    d_qdo = lax.ppermute(qdo, "t", d_pairs)
    s_out, s_dq, s_dk, s_dv, part_x, stats = call(
        self_kernel, "selfatt", 1, [shape(TOK, F32)] * 4 + [shape(2 * TOK, BF16), shape(16, F32, TOK)],
        scal, sums, gains, sq_later, sk, sv, do, s_x, s_d, flops=12 * HEADS * TOK * 3 * TOK * DH,
    )
    stats, d_qdo = lax.optimization_barrier((stats, d_qdo))
    d_stats = lax.ppermute(stats, "t", d_pairs)
    back_x = lax.ppermute(part_x, "t", x_pairs)
    s_dk, s_dv = call(
        key_side_kernel, "keyside", 1, [shape(TOK, F32)] * 2,
        scal, sums, gains, sk, sv, d_qdo, d_stats, s_dk, s_dv, flops=8 * HEADS * TOK * TOK * DH,
    )
    att = (s_out + c_out).astype(BF16)
    svg, cvg, dks, dkc, inner = call(
        gather_kernel, "gather", 1, [shape(TOK, BF16)] * 2 + [shape(TOK, F32)] * 2 + [shape(8, F32, TOK)],
        scal, gains, sq, sk, cq, ck, s_dq, c_dq, s_dk, s_dv, c_back[0], c_back[1], c_back[2], back_x,
    )
    inner = lax.all_gather(inner, "head")
    g0, g1, g2, g3 = call(
        final_kernel, "final", 1, [shape(TOK, BF16)] * 4, scal, gains, sums, inner, sq, sk, cq, ck, s_dq, dks, c_dq, dkc
    )
    return att, g0, g1, svg, g2, g3, cvg


def solution(mesh):
    seq = mesh.shape["seq"]
    grid = Mesh(mesh.devices.reshape(4, seq // 4, mesh.shape["head"]), ("y", "t", "head"))
    block = P(("y", "t"), "head")
    return jax.shard_map(
        on_device,
        mesh=grid,
        in_specs=(block,) * 7 + (P(None, None, "head"), P()),
        out_specs=(block,) * 7,
        check_vma=False,
    )
```

```python
import functools

import jax
import jax.numpy as jnp
from jax import lax
from jax.experimental import pallas as pl
from jax.experimental.pallas import tpu as pltpu
from jax.sharding import Mesh, PartitionSpec as P

DH = 128
BLK = 64
WIDTH = 1536
NSUB = 4
HEADS = 3
TOK = 256
COLS = 384
COLUMNS = [slice(h * DH, (h + 1) * DH) for h in range(HEADS)]
EPSILON = 1e-06
SCALE = DH ** (-0.5)
MASKED = -1e30
LOG2E = 1.4426950408889634
F32 = jnp.float32
BF16 = jnp.bfloat16
VMEM = pltpu.VMEM
VSPEC = pl.BlockSpec(memory_space=pltpu.VMEM)
SSPEC = pl.BlockSpec(memory_space=pltpu.SMEM)


def dot(a, b, ca, cb):
    return lax.dot_general(a, b, (((ca,), (cb,)), ((), ())), preferred_element_type=F32)


def row_sums(product):
    folded = product[:, 0:128] + product[:, 128:256] + product[:, 256:384]
    return jnp.sum(jnp.transpose(folded), axis=0, keepdims=True)


def squares_kernel(*refs):
    ins, out = refs[:4], refs[-1]
    out[...] = jnp.zeros(out.shape, F32)
    for i, ref in enumerate(ins):
        wide = ref[0:TOK, :].astype(F32)
        out[i : i + 1, :] = row_sums(wide * wide)


def more_squares_kernel(own, *refs):
    ins, out = refs[:-1], refs[-1]
    out[0:8, :] = own[...]
    out[8:16, :] = jnp.zeros((8, TOK), F32)
    for i, ref in enumerate(ins):
        wide = ref[0:TOK, :].astype(F32)
        row = (8, 4, 7, 6, 5)[i]
        out[row : row + 1, :] = row_sums(wide * wide)


def attend(qs, kns, vs, dos, valid, masks, key_side=3):
    heads, blocks = range(len(qs)), range(len(kns[0]))
    scores = [[dot(kns[h][j], qs[h], 1, 1) for j in blocks] for h in heads]
    if masks is not None:
        scores = [[jnp.where(masks[j], scores[h][j], MASKED) for j in blocks] for h in heads]
    dprobs = [[dot(vs[h][j], dos[h], 1, 1) for j in blocks] for h in heads]
    tops = []
    for h in heads:
        peaks = [jnp.max(scores[h][j], axis=0, keepdims=True) for j in blocks]
        if valid is not None:
            peaks = [peaks[0]] + [jnp.where(ok, peak, MASKED) for ok, peak in zip(valid[1:], peaks[1:])]
        tops.append(functools.reduce(jnp.maximum, peaks))
    if valid is None:
        lifts = [[tops[h]] * len(blocks) for h in heads]
    else:
        lifts = [[tops[h]] + [jnp.where(ok, tops[h], -MASKED) for ok in valid[1:]] for h in heads]
    shifted = [[jnp.exp2((scores[h][j] - lifts[h][j]) * (SCALE * LOG2E)) for j in blocks] for h in heads]
    inverse = [1.0 / sum(jnp.sum(e, axis=0, keepdims=True) for e in shifted[h]) for h in heads]
    probs = [[e * inverse[h] for e in shifted[h]] for h in heads]
    weights = [[p.astype(BF16) for p in probs[h]] for h in heads]
    delta = [sum(jnp.sum(p * d, axis=0, keepdims=True) for p, d in zip(probs[h], dprobs[h])) for h in heads]
    dscores = [
        [(p * (d - delta[h]) * SCALE).astype(BF16) for p, d in zip(probs[h], dprobs[h])] for h in heads
    ]
    results = []
    for h in heads:
        out = sum(dot(w, v, 0, 0) for w, v in zip(weights[h], vs[h]))
        dq = sum(dot(ds, kn, 0, 0) for ds, kn in zip(dscores[h], kns[h]))
        dks = [dot(ds, qs[h], 1, 0) for ds in dscores[h][:key_side]]
        dvs = [dot(w, dos[h], 1, 0) for w in weights[h][:key_side]]
        results.append((out, dq, dks, dvs, (tops[h], inverse[h], delta[h])))
    return results


def over_heads(ref):
    return ref[0] + ref[1] + ref[2] + ref[3]


def inverse_rms(sums_ref):
    return jnp.transpose(lax.rsqrt(over_heads(sums_ref) * (1.0 / WIDTH) + EPSILON))


def normed(raw, inv, gain):
    return (raw.astype(F32) * inv * gain).astype(BF16)


def self_kernel(
    scal, sums, gains, q_ref, k_ref, v_ref, do_ref, x_ref, d_ref,
    out_ref, dq_ref, dk_ref, dv_ref, px_ref, stats,
):
    group, slot = scal[0], scal[1]
    tower = (group == 3).astype(jnp.int32)
    inv = inverse_rms(sums)
    qs, kns, vs, dos = [], [], [], []
    for c in COLUMNS:
        gk = gains[tower, 1:2, c]
        qs.append(normed(q_ref[:, c], inv[:, 0:1], gains[tower, 0:1, c]))
        kns.append(
            [
                normed(k_ref[:, c], inv[:, 1:2], gk),
                normed(x_ref[0:TOK, c], inv[:, 5:6], gk),
                normed(d_ref[0:TOK, c], inv[:, 4:5], gk),
            ]
        )
        vs.append([v_ref[:, c], x_ref[TOK:, c], d_ref[TOK:, c]])
        dos.append(do_ref[:, c])
    has_d = (slot > 0) & (slot < 31)
    results = attend(qs, kns, vs, dos, [True, True, has_d], None, key_side=2)
    stats[...] = jnp.zeros(stats.shape, F32)
    stats[9:10, :] = lax.rsqrt(over_heads(sums)[0:1, :] * (1.0 / WIDTH) + EPSILON)
    for h, (c, (out, dq, dks, dvs, rows)) in enumerate(zip(COLUMNS, results)):
        out_ref[:, c] = out
        dq_ref[:, c] = dq
        dk_ref[:, c] = dks[0]
        dv_ref[:, c] = dvs[0]
        px_ref[0:TOK, c] = dks[1].astype(BF16)
        px_ref[TOK:, c] = dvs[1].astype(BF16)
        for i, row in enumerate(rows):
            stats[3 * i + h : 3 * i + h + 1, :] = row


def key_side_kernel(scal, sums, gains, k_ref, v_ref, qdo_ref, stats, dk_in, dv_in, dk_ref, dv_ref):
    tower = (scal[0] == 3).astype(jnp.int32)
    inv_k = inverse_rms(sums)[:, 1:2]
    inv_q = jnp.transpose(stats[...])[:, 9:10]
    kns = [normed(k_ref[:, c], inv_k, gains[tower, 1:2, c]) for c in COLUMNS]
    qs = [normed(qdo_ref[0:TOK, c], inv_q, gains[tower, 0:1, c]) for c in COLUMNS]
    dos = [qdo_ref[TOK:, c] for c in COLUMNS]
    scores = [dot(kn, q, 1, 1) for kn, q in zip(kns, qs)]
    dprobs = [dot(v_ref[:, c], do, 1, 1) for c, do in zip(COLUMNS, dos)]
    for h, c in enumerate(COLUMNS):
        top, inverse, delta = (stats[3 * i + h : 3 * i + h + 1, :] for i in range(3))
        p = jnp.exp2((scores[h] - top) * (SCALE * LOG2E)) * inverse
        ds = (p * (dprobs[h] - delta) * SCALE).astype(BF16)
        dk_ref[:, c] = dk_in[:, c] + dot(ds, qs[h], 1, 0)
        dv_ref[:, c] = dv_in[:, c] + dot(p.astype(BF16), dos[h], 1, 0)


def cross_kernel(
    scal, sums, gains, q_ref, do_ref, i0, i1, i2,
    out_ref, dq_ref, p0, p1, p2,
):
    group = scal[0]
    audio = group == 3
    inv = inverse_rms(sums)
    sub_row = lax.broadcasted_iota(jnp.int32, (1, TOK), 1) // BLK
    sub_col = lax.broadcasted_iota(jnp.int32, (TOK, 1), 0) // BLK

    def spread(base, offset, sub):
        value = jnp.zeros(sub.shape, jnp.int32)
        for b in range(NSUB):
            value = jnp.where(sub == b, scal[base + 2 * b + offset], value)
        return value

    @pl.when(audio)
    def _():
        masks = []
        for j in range(3):
            lower = spread(2 + 8 * j, 0, sub_col)
            upper = spread(2 + 8 * j, 1, sub_col)
            masks.append((sub_row >= lower) & (sub_row < upper))
        qs = [normed(q_ref[:, c], inv[:, 2:3], gains[1, 2:3, c]) for c in COLUMNS]
        dos = [do_ref[:, c] for c in COLUMNS]
        kns = [
            [normed(r[0:TOK, c], inv[:, 6 + j : 7 + j], gains[0, 3:4, c]) for j, r in enumerate((i0, i1, i2))]
            for c in COLUMNS
        ]
        vs = [[r[TOK:, c] for r in (i0, i1, i2)] for c in COLUMNS]
        for c, (out, dq, dks, dvs, _) in zip(COLUMNS, attend(qs, kns, vs, dos, None, masks)):
            out_ref[:, c] = out
            dq_ref[:, c] = dq
            for ref, dk, dv in zip((p0, p1, p2), dks, dvs):
                ref[0:TOK, c] = dk.astype(BF16)
                ref[TOK:, c] = dv.astype(BF16)

    @pl.when(jnp.logical_not(audio))
    def _():
        base = 2 + 8 * group
        lower = spread(base, 0, sub_row)
        upper = spread(base, 1, sub_row)
        mask = (sub_col >= lower) & (sub_col < upper)
        first, second = group == 0, group == 1

        def pick(a, b, c):
            return jnp.where(first, a, jnp.where(second, b, c))

        inv_k = pick(inv[:, 6:7], inv[:, 7:8], inv[:, 8:9])
        qs = [normed(q_ref[:, c], inv[:, 2:3], gains[0, 2:3, c]) for c in COLUMNS]
        dos = [do_ref[:, c] for c in COLUMNS]
        kns = [
            [normed(pick(i0[0:TOK, c], i1[0:TOK, c], i2[0:TOK, c]), inv_k, gains[1, 3:4, c])] for c in COLUMNS
        ]
        vs = [[pick(i0[TOK:, c], i1[TOK:, c], i2[TOK:, c])] for c in COLUMNS]
        for c, (out, dq, dks, dvs, _) in zip(COLUMNS, attend(qs, kns, vs, dos, None, [mask])):
            out_ref[:, c] = out
            dq_ref[:, c] = dq
            dk = dks[0].astype(BF16)
            dv = dvs[0].astype(BF16)
            for ref in (p0, p1, p2):
                ref[0:TOK, c] = dk
                ref[TOK:, c] = dv


def gather_kernel(
    scal, gains, sq, sk, cq, ck, sdq, cdq, sdk, sdv, r1, r0, r2, rx,
    svg, cvg, dks_ref, dkc_ref, inner,
):
    tower = (scal[0] == 3).astype(jnp.int32)
    dkc = r0[0:TOK, :].astype(F32) + r1[0:TOK, :].astype(F32) + r2[0:TOK, :].astype(F32)
    cvg[...] = (r0[TOK:, :].astype(F32) + r1[TOK:, :].astype(F32) + r2[TOK:, :].astype(F32)).astype(BF16)
    dks = sdk[...] + rx[0:TOK, :].astype(F32)
    svg[...] = (sdv[...] + rx[TOK:, :].astype(F32)).astype(BF16)
    dks_ref[...] = dks
    dkc_ref[...] = dkc
    inner[...] = jnp.zeros(inner.shape, F32)
    for i, (x, y) in enumerate(((sq, sdq[...]), (sk, dks), (cq, cdq[...]), (ck, dkc))):
        inner[i : i + 1, :] = row_sums(gains[tower, i : i + 1, :] * y * x[...].astype(F32))


def final_kernel(scal, gains, sums, inner, sq, sk, cq, ck, y0, y1, y2, y3, o0, o1, o2, o3):
    tower = (scal[0] == 3).astype(jnp.int32)
    inv = inverse_rms(sums)
    mean = jnp.transpose(over_heads(inner)) * (1.0 / WIDTH)
    for i, (x, y, o) in enumerate(zip((sq, sk, cq, ck), (y0, y1, y2, y3), (o0, o1, o2, o3))):
        r = inv[:, i : i + 1]
        o[...] = (
            r * gains[tower, i : i + 1, :] * y[...] - x[...].astype(F32) * (r * r * r * mean[:, i : i + 1])
        ).astype(BF16)


def shape(rows, dtype, cols=COLS):
    return jax.ShapeDtypeStruct((rows, cols), dtype)


def call(kernel, name, scalars, outs, *args, flops=0):
    nbytes = sum(a.size * a.dtype.itemsize for a in args) + sum(o.size * o.dtype.itemsize for o in outs)
    return pl.pallas_call(
        kernel,
        name=name,
        out_shape=outs,
        in_specs=[SSPEC] * scalars + [VSPEC] * (len(args) - scalars),
        out_specs=[VSPEC] * len(outs),
        compiler_params=pltpu.CompilerParams(vmem_limit_bytes=40 * 1024 * 1024),
        cost_estimate=pl.CostEstimate(flops=flops, bytes_accessed=nbytes, transcendentals=0),
    )(*args)


def on_device(sq, sk, sv, cq, ck, cv, do, gains, span):
    group = lax.axis_index("y")
    slot = lax.axis_index("t")
    slots = lax.axis_size("t")
    x_pairs = [(i, i ^ 1) for i in range(slots)]
    d_pairs = [(i, i + 1) if i % 2 else (i, i - 1) for i in range(1, slots - 1)]
    pairs = [[(3, j), (j, 3)] for j in range(3)]
    spans = lax.dynamic_slice_in_dim(span.reshape(3, NSUB * slots, 2), slot * NSUB, NSUB, 1)
    scal = jnp.concatenate([jnp.stack([group, slot]).astype(jnp.int32), spans.reshape(-1)])

    s_kv, c_kv = jnp.concatenate([sk, sv]), jnp.concatenate([ck, cv])
    scal, sq = lax.optimization_barrier((scal, sq))
    own = call(squares_kernel, "squares", 0, [shape(8, F32, TOK)], sq, sk, cq, ck, do, sv, gains)[0]
    c_in = [None] * 3
    s_x = lax.ppermute(s_kv, "t", x_pairs)
    c_in[1] = lax.ppermute(c_kv, "y", pairs[1])
    c_in[0] = lax.ppermute(c_kv, "y", pairs[0])
    s_later, s_x = lax.optimization_barrier((s_kv, s_x))
    s_d = lax.ppermute(s_later, "t", d_pairs)
    c_in[2] = lax.ppermute(c_kv, "y", pairs[2])
    qdo, own = lax.optimization_barrier((jnp.concatenate([sq, do]), own))
    sums = call(
        more_squares_kernel, "more", 0, [shape(16, F32, TOK)], own, c_in[2], s_d, c_in[1], c_in[0], s_x
    )[0]
    sums = lax.all_gather(sums, "head")

    c_out, c_dq, *c_parts = call(
        cross_kernel, "cross", 1, [shape(TOK, F32)] * 2 + [shape(2 * TOK, BF16)] * 3,
        scal, sums, gains, cq, do, *c_in, flops=12 * HEADS * TOK * 3 * TOK * DH,
    )
    c_back = [None] * 3
    for j in (1, 0, 2):
        c_back[j] = lax.ppermute(c_parts[j], "y", pairs[j])
    sq_later, qdo, c_out = lax.optimization_barrier((sq, qdo, c_out))
    d_qdo = lax.ppermute(qdo, "t", d_pairs)
    s_out, s_dq, s_dk, s_dv, part_x, stats = call(
        self_kernel, "selfatt", 1, [shape(TOK, F32)] * 4 + [shape(2 * TOK, BF16), shape(16, F32, TOK)],
        scal, sums, gains, sq_later, sk, sv, do, s_x, s_d, flops=12 * HEADS * TOK * 3 * TOK * DH,
    )
    stats, d_qdo = lax.optimization_barrier((stats, d_qdo))
    d_stats = lax.ppermute(stats, "t", d_pairs)
    back_x = lax.ppermute(part_x, "t", x_pairs)
    s_dk, s_dv = call(
        key_side_kernel, "keyside", 1, [shape(TOK, F32)] * 2,
        scal, sums, gains, sk, sv, d_qdo, d_stats, s_dk, s_dv, flops=8 * HEADS * TOK * TOK * DH,
    )
    att = (s_out + c_out).astype(BF16)
    svg, cvg, dks, dkc, inner = call(
        gather_kernel, "gather", 1, [shape(TOK, BF16)] * 2 + [shape(TOK, F32)] * 2 + [shape(8, F32, TOK)],
        scal, gains, sq, sk, cq, ck, s_dq, c_dq, s_dk, s_dv, c_back[1], c_back[0], c_back[2], back_x,
    )
    inner = lax.all_gather(inner, "head")
    g0, g1, g2, g3 = call(
        final_kernel, "final", 1, [shape(TOK, BF16)] * 4, scal, gains, sums, inner, sq, sk, cq, ck, s_dq, dks, c_dq, dkc
    )
    return att, g0, g1, svg, g2, g3, cvg


def solution(mesh):
    seq = mesh.shape["seq"]
    grid = Mesh(mesh.devices.reshape(4, seq // 4, mesh.shape["head"]), ("y", "t", "head"))
    block = P(("y", "t"), "head")
    return jax.shard_map(
        on_device,
        mesh=grid,
        in_specs=(block,) * 7 + (P(None, None, "head"), P()),
        out_specs=(block,) * 7,
        check_vma=False,
    )
```
